128 devices in a mesh: lat: 32 (over z, x, core), lon: 4 (over y).
Axes of the slice: x: 4, y: 4, z: 4, core: 2. Of those that a mesh axis runs over, the one named last changes fastest.
Arguments:
- state: float32 [512, 1440, 256], P('lat', 'lon'), may hold values from -6 to 6
- winds: bfloat16 [512, 1440, 128], P('lat', 'lon'), may hold values from -0.44921875 to 0.44921875
- decay: float32 [4], replicated, may hold values from 0.005 to 0.5
- widths: int32 [512], replicated, may hold values from 0 to 480, as said below
Outputs:
- advected: bfloat16 [512, 1440, 256], P('lat', 'lon')
The draws below stay inside these ranges and needn't reach their ends.
Inputs may be any that keep to these rules, and one draw needn't show every extreme that they name: widths is 0 on rows 128 to 383 and at least 1 on the other rows; the first and last rows have exactly 480.
All inputs are finite; a program needn't handle non-finite values.
Results may differ from the reference program's by a relative error of at most 0.0075.
Values may be sent and summed in bfloat16 or wider, within the bound.
A program may use at most 128 MiB of HBM per device.

```python
import math
import jax
import jax.numpy as jnp
from jax import lax

NLON = 1440
LEVELS = 64
FIELDS = 4
HMAX = 480
ADV_STEPS = 4
NLAT = 512


def draw_widths(key, part):
    index = jnp.arange(NLAT)
    quarter = NLAT // 4
    depth = jnp.where(index < quarter, quarter - index, jnp.where(index >= 3 * quarter, index - 3 * quarter + 1, 0))
    base = 1 + (depth - 1) * (HMAX - 1) // max(quarter - 1, 1)
    jitter = jax.random.randint(key, (NLAT,), 0, 3)
    width = jnp.where(depth == quarter, HMAX, jnp.minimum(base + jitter, HMAX))
    return jnp.where(depth > 0, width, 0).astype(jnp.int32)


def level_of(key, shape, pieces, least, top_value):
    def one(dim, shards_of):
        draws = jax.random.uniform(jax.random.fold_in(jax.random.fold_in(key, 6), dim), (shards_of,), jnp.float32, least / len(pieces), top_value / len(pieces))
        return jnp.repeat(jnp.exp(draws), shape[dim] // shards_of).reshape((-1,) + (1,) * (len(shape) - dim - 1))

    loudness = one(*pieces[0])
    for cut in pieces[1:]:
        loudness = loudness * one(*cut)
    return loudness


def centred(stream_key, dims, deviation, limit, split=(), dtype=jnp.bfloat16):
    level = level_of(stream_key, dims, split, -0.22, 0.18) if split else 1.0
    drawn = jax.random.normal(stream_key, dims, jnp.float32) * deviation * level
    return jnp.minimum(jnp.maximum(drawn, -limit), limit).astype(dtype)


def setup_inputs(seed: int = 0) -> dict:
    splits = jax.random.split(jax.random.key(seed), 5)
    state = centred(splits[0], (NLAT, NLON, FIELDS * LEVELS), 1.0, 6.0, ((0, 32), (1, 4)), jnp.float32)
    winds = jnp.clip(jax.random.uniform(splits[1], (NLAT, NLON, 2 * LEVELS), jnp.float32, -0.44921875, 0.44921875) * level_of(splits[1], (NLAT, NLON, 2 * LEVELS), ((0, 32), (1, 4)), -0.4, 0.0), -0.44921875, 0.44921875).astype(jnp.bfloat16)
    decay = jnp.clip(jnp.exp(jax.random.uniform(splits[2], (FIELDS,), jnp.float32, math.log(0.005), math.log(0.5))), 0.005, 0.5)
    widths = draw_widths(jax.random.fold_in(splits[4], 71), 0)
    return dict(state=state, winds=winds, decay=decay, widths=widths)


def smooth(rows, row_widths, decay):
    low = rows.astype(jnp.bfloat16)
    offsets = jnp.arange(NLON)
    gap = jnp.abs(offsets[:, None] - offsets[None, :])
    gap = jnp.minimum(gap, NLON - gap).astype(jnp.float32)
    first_gap = jnp.minimum(offsets, NLON - offsets).astype(jnp.float32)

    def one_row(item):
        row, width = item
        reach = width.astype(jnp.float32)
        kernel = jnp.where(gap[None] <= reach, jnp.exp(-decay[:, None, None] * gap[None]), 0.0)
        totals = jnp.sum(jnp.where(first_gap[None] <= reach, jnp.exp(-decay[:, None] * first_gap[None]), 0.0), axis=1)
        matrix = (kernel / totals[:, None, None]).astype(jnp.bfloat16)
        shaped = row.reshape(NLON, FIELDS, LEVELS).astype(jnp.float32)
        result = jnp.einsum("fij,ifl->jfl", matrix.astype(jnp.float32), shaped)
        return result.reshape(NLON, FIELDS * LEVELS).astype(jnp.bfloat16)

    return lax.map(one_row, (low, row_widths))


def advect(field, east_courant, north_courant):
    rows = field.shape[0]
    cols = field.shape[1]
    lat_ext = jnp.pad(field, ((2, 2), (0, 0), (0, 0)))
    lon_ext = jnp.concatenate([field[:, -2:], field, field[:, :2]], axis=1)
    north_one = lat_ext[3:rows + 3]
    south_one = lat_ext[1:rows + 1]
    north_two = lat_ext[4:rows + 4]
    south_two = lat_ext[0:rows]
    east_one = lon_ext[:, 3:cols + 3]
    west_one = lon_ext[:, 1:cols + 1]
    east_two = lon_ext[:, 4:cols + 4]
    west_two = lon_ext[:, 0:cols]
    first_x = (8.0 * (east_one - west_one) - (east_two - west_two)) / 12.0
    second_x = (16.0 * (east_one + west_one) - (east_two + west_two) - 30.0 * field) / 12.0
    first_y = (8.0 * (north_one - south_one) - (north_two - south_two)) / 12.0
    second_y = (16.0 * (north_one + south_one) - (north_two + south_two) - 30.0 * field) / 12.0
    return (field - east_courant * first_x + 0.5 * east_courant * east_courant * second_x
            - north_courant * first_y + 0.5 * north_courant * north_courant * second_y)


def reference(state, winds, decay, widths):
    quarter = NLAT // 4
    polar_rows = jnp.concatenate([state[:quarter], state[3 * quarter:]], axis=0)
    polar_widths = jnp.concatenate([widths[:quarter], widths[3 * quarter:]], axis=0)
    smoothed = smooth(polar_rows, polar_widths, decay).astype(jnp.float32)
    field = jnp.concatenate([smoothed[:quarter], state[quarter:3 * quarter], smoothed[quarter:]], axis=0)
    east_courant = jnp.tile(winds[:, :, :LEVELS].astype(jnp.float32), (1, 1, FIELDS))
    north_courant = jnp.tile(winds[:, :, LEVELS:].astype(jnp.float32), (1, 1, FIELDS))
    for step in range(ADV_STEPS):
        field = advect(field, east_courant, north_courant)
    return field.astype(jnp.bfloat16)
```

```python
import functools

import jax
import jax.numpy as jnp
from jax import lax
from jax.experimental import pallas as pl
from jax.experimental.pallas import tpu as pltpu
from jax.sharding import PartitionSpec as P

STEPS = 4
HALO = 2 * STEPS
MESH = pl.DeviceIdType.MESH
F32 = jnp.float32
BF16 = jnp.bfloat16
FAR = 1.0e6


def filter_kernel(
    dims, state, winds, decay, widths, ext, wext,
    stf, low, circ, gaps, table, mat, xs, yc, ot, wide, wv, wasm, wedge, wland, easm, eedge, eland, zero,
    ld, fs, fr, rs, rr, hs, hr, wsem, els, elr, wrow_s, wrow_r, loc,
):
    bands, rows, cols, pad, levels = dims
    half = 2 * levels
    lat = lax.axis_index("lat")
    lon = lax.axis_index("lon")
    quarter = bands // 4
    polar = (lat < quarter) | (lat >= bands - quarter)
    twin = jnp.where((lat // quarter) % 2 == 0, lat + quarter, lat - quarter)
    home = jnp.where(polar, lat, twin)
    has_south = lat > 0
    has_north = lat < bands - 1

    def at(la, lo):
        return {"lat": la, "lon": lo}

    def remote(src, dst, send, recv, la, lo):
        return pltpu.make_async_remote_copy(
            src_ref=src, dst_ref=dst, send_sem=send, recv_sem=recv, device_id=at(la, lo), device_id_type=MESH
        )

    barrier = pltpu.get_barrier_semaphore()
    for k in range(4):
        pl.semaphore_signal(barrier, inc=1, device_id=at(twin, (lon + k) % 4), device_id_type=MESH)
        if k:
            pl.semaphore_signal(barrier, inc=1, device_id=at(lat, (lon + k) % 4), device_id_type=MESH)

    for side in (1, bands - 1):
        pl.semaphore_signal(barrier, inc=1, device_id=at((lat + side) % bands, lon), device_id_type=MESH)

    order = []
    for g in range(2):
        for k in (2, 1, 3, 0):
            for part in (1, 0):
                order.append((g, k, part))

    def row_of(g, k, part):
        return 8 * part + 4 * g + (lon + k) % 4

    for g, k, part in order:
        i = row_of(g, k, part)
        pltpu.make_async_copy(state.at[i], stf.at[i], ld.at[i]).start()
    pltpu.make_async_copy(winds, wv, wsem.at[0]).start()

    pl.semaphore_wait(barrier, 9)

    def forward(g, h, k, part, i):
        src = low.at[i, h]
        dst = circ.at[g, h, lon]
        return remote(src, dst, fs.at[i, h], fr.at[g, h, lon], twin if part else lat, (lon + k) % 4)

    @pl.when(polar)
    def _():
        for g in range(2):
            for h in range(2):
                for k in (2, 1, 3, 0):
                    for part in (1, 0):
                        i = row_of(g, k, part)
                        if h == 0:
                            pltpu.make_async_copy(state.at[i], stf.at[i], ld.at[i]).wait()
                            low[i, 0] = stf[i, :, :half].astype(BF16)
                            low[i, 1] = stf[i, :, half:].astype(BF16)
                        if k == 0 and part == 0:
                            pltpu.make_async_copy(low.at[i, h], circ.at[g, h, lon], fr.at[g, h, lon]).start()
                        else:
                            forward(g, h, k, part, i).start()

    pltpu.make_async_copy(winds, wv, wsem.at[0]).wait()
    wedge[0] = wv[:, 0:16, :]
    wedge[1] = wv[:, cols - 16 : cols, :]

    def wind_edge(n):
        return remote(wedge.at[n], wland.at[n], wsem.at[1 + n], wsem.at[3 + n], lat, (lon + (3 if n == 0 else 1)) % 4)

    for n in range(2):
        wind_edge(n).start()

    def state_edge(n):
        return remote(eedge.at[n], eland.at[n], els.at[n], elr.at[n], lat, (lon + (3 if n == 0 else 1)) % 4)

    @pl.when(jnp.logical_not(polar))
    def _():
        def load(i, c):
            pltpu.make_async_copy(state.at[i], stf.at[i], ld.at[i]).wait()
            for h in range(2):
                lanes = slice(h * half, (h + 1) * half)
                eedge[0, i, h] = stf[i, 0:16, lanes].astype(BF16)
                eedge[1, i, h] = stf[i, cols - 16 : cols, lanes].astype(BF16)
            return c

        lax.fori_loop(0, rows, load, 0)
        for n in range(2):
            state_edge(n).start()

    zero[...] = jnp.zeros(zero.shape, BF16)

    @pl.when(jnp.logical_not(has_south))
    def _():
        pltpu.make_async_copy(zero, ext.at[pl.ds(0, HALO)], loc.at[2]).start()
        pltpu.make_async_copy(zero.at[:, 0], wext.at[pl.ds(0, HALO)], loc.at[3]).start()

    @pl.when(jnp.logical_not(has_north))
    def _():
        pltpu.make_async_copy(zero, ext.at[pl.ds(rows + HALO, HALO)], loc.at[2]).start()
        pltpu.make_async_copy(zero.at[:, 0], wext.at[pl.ds(rows + HALO, HALO)], loc.at[3]).start()

    for n in range(2):
        wind_edge(n).wait()

    def assemble(i, c):
        wide[0, 0:8] = wland[1, i, 8:16, :].astype(F32)
        wide[0, pl.ds(8, cols)] = wv[i].astype(F32)
        wide[0, pl.ds(8 + cols, 16)] = wland[0, i].astype(F32)
        wasm[i] = wide[0].astype(BF16)
        return c

    lax.fori_loop(0, rows, assemble, 0)

    def wind_rows(n):
        if n == 0:
            return remote(wasm.at[pl.ds(0, HALO)], wext.at[pl.ds(rows + HALO, HALO)], wrow_s.at[0], wrow_r.at[1], lat - 1, lon)
        return remote(wasm.at[pl.ds(rows - HALO, HALO)], wext.at[pl.ds(0, HALO)], wrow_s.at[1], wrow_r.at[0], lat + 1, lon)

    @pl.when(has_south)
    def _():
        wind_rows(0).start()

    @pl.when(has_north)
    def _():
        wind_rows(1).start()

    wind_local = pltpu.make_async_copy(wasm, wext.at[pl.ds(HALO, rows)], loc.at[0])
    wind_local.start()

    def to_south(src, i, h):
        return remote(src, ext.at[rows + HALO + i, h], hs.at[i, h], hr.at[8 + i, h], lat - 1, lon)

    def to_north(src, i, h):
        return remote(src, ext.at[i - 8, h], hs.at[i, h], hr.at[i - 8, h], lat + 1, lon)

    state_local = pltpu.make_async_copy(easm, ext.at[pl.ds(HALO, rows)], loc.at[1])

    @pl.when(jnp.logical_not(polar))
    def _():
        for n in range(2):
            state_edge(n).wait()

        def assemble_state(i, c):
            for h in range(2):
                lanes = slice(h * half, (h + 1) * half)
                wide[h, 0:8] = eland[1, i, h, 8:16, :].astype(F32)
                wide[h, pl.ds(8, cols)] = stf[i, :, lanes]
                wide[h, pl.ds(8 + cols, 16)] = eland[0, i, h].astype(F32)
                easm[i, h] = wide[h].astype(BF16)
            return c

        lax.fori_loop(0, rows, assemble_state, 0)

        def south(i, c):
            for h in range(2):
                to_south(easm.at[i, h], i, h).start()
            return c

        def north(i, c):
            for h in range(2):
                to_north(easm.at[i, h], i, h).start()
            return c

        lax.fori_loop(0, 8, south, 0)
        lax.fori_loop(8, 16, north, 0)
        state_local.start()

    far = lax.broadcasted_iota(jnp.int32, (cols, pad), 0)
    near = lax.broadcasted_iota(jnp.int32, (cols, pad), 1)
    for d in range(4):
        apart = jnp.abs(far - near - d * cols)
        apart = jnp.minimum(apart, 4 * cols - apart).astype(F32)
        gaps[d] = jnp.where(near < cols, apart, FAR)

    def tabulate(n, c):
        f, d = n // 4, n % 4
        table[f, d] = jnp.exp(-decay[f] * gaps[d])
        return c

    lax.fori_loop(0, 16, tabulate, 0)
    for d in range(4):
        xs[d, pl.ds(pad - 32, 32)] = jnp.zeros((32, 4 * levels), BF16)

    def returned(u, k):
        g, h = u // 2, u % 2
        i = jnp.where(polar, 0, 8) + 4 * g + lon
        t = (lon + k) % 4
        return (
            remote(ot.at[u, t], ext.at[HALO + i, h], rs.at[u, k], rr.at[i, h], home, t),
            pltpu.make_async_copy(ot.at[u, t], ext.at[HALO + i, h], rr.at[i, h]),
        )

    def unit(u, c):
        g, h = u // 2, u % 2
        i = jnp.where(polar, 0, 8) + 4 * g + lon
        reach = widths[home * rows + i].astype(F32)
        for t in range(4):
            pltpu.make_async_copy(low.at[0, 0], circ.at[g, h, t], fr.at[g, h, t]).wait()
        for ff in range(2):
            f = 2 * h + ff
            total = jnp.zeros((1, 1), F32)
            for d in range(4):
                kept = jnp.where(gaps[d, 0:1] <= reach, table[f, d, 0:1], 0.0)
                total = total + jnp.sum(kept, axis=1, keepdims=True)
            scale = 1.0 / total
            for d in range(4):
                mat[d] = jnp.where(gaps[d] <= reach, table[f, d] * scale, 0.0).astype(BF16)
                xs[d, pl.ds(0, cols)] = jnp.concatenate(
                    [circ[g, h, (t + d) % 4, :, ff * levels : (ff + 1) * levels] for t in range(4)], axis=1
                )
            result = jnp.dot(mat[0], xs[0], preferred_element_type=F32)
            for d in range(1, 4):
                result = result + jnp.dot(mat[d], xs[d], preferred_element_type=F32)
            for t in range(4):
                yc[pl.ds(8 + t * cols, cols), ff * levels : (ff + 1) * levels] = result[:, t * levels : (t + 1) * levels]
        yc[0:8] = yc[pl.ds(4 * cols, 8)]
        yc[pl.ds(8 + 4 * cols, 16)] = yc[8:24]
        for t in range(4):
            ot[u, t] = yc[pl.ds(t * cols, pad)].astype(BF16)
        for k in (2, 1, 3):
            returned(u, k)[0].start()

        @pl.when(polar)
        def _():
            returned(u, 0)[1].start()

        @pl.when(jnp.logical_not(polar))
        def _():
            returned(u, 0)[0].start()

        return c

    def pass_on(u):
        g, h = u // 2, u % 2

        @pl.when(polar)
        def _():
            def south(q, c):
                i = 4 * g + q
                pltpu.make_async_copy(ot.at[0, 0], ext.at[HALO + i, h], rr.at[i, h]).wait()

                @pl.when(has_south)
                def _():
                    to_south(ext.at[HALO + i, h], i, h).start()

                return c

            def north(q, c):
                i = 8 + 4 * g + q
                pltpu.make_async_copy(ot.at[0, 0], ext.at[HALO + i, h], rr.at[i, h]).wait()

                @pl.when(has_north)
                def _():
                    to_north(ext.at[HALO + i, h], i, h).start()

                return c

            lax.fori_loop(0, 4, south, 0)
            lax.fori_loop(0, 4, north, 0)

    def stage(n, c):
        @pl.when(n < 4)
        def _():
            unit(n, 0)

        @pl.when(n >= 2)
        def _():
            pass_on(n - 2)

        return c

    lax.fori_loop(0, 6, stage, 0)

    wind_local.wait()

    @pl.when(jnp.logical_not(polar))
    def _():
        state_local.wait()

    @pl.when(polar)
    def _():
        for g in range(2):
            for h in range(2):
                for k in (2, 1, 3, 0):
                    for part in (1, 0):
                        if not (k == 0 and part == 0):
                            forward(g, h, k, part, row_of(g, k, part)).wait_send()

    def sent(u, c):
        for k in (1, 2, 3):
            returned(u, k)[0].wait_send()

        @pl.when(jnp.logical_not(polar))
        def _():
            returned(u, 0)[0].wait_send()

        return c

    lax.fori_loop(0, 4, sent, 0)

    @pl.when(has_south)
    def _():
        wind_rows(0).wait_send()
        wind_rows(1).wait_recv()

        def each(i, c):
            for h in range(2):
                to_south(ext.at[HALO + i, h], i, h).wait_send()
                to_north(ext.at[HALO + i, h], i + 8, h).wait_recv()
            return c

        lax.fori_loop(0, 8, each, 0)

    @pl.when(has_north)
    def _():
        wind_rows(1).wait_send()
        wind_rows(0).wait_recv()

        def each(i, c):
            for h in range(2):
                to_north(ext.at[HALO + i, h], i + 8, h).wait_send()
                to_south(ext.at[HALO + i, h], i, h).wait_recv()
            return c

        lax.fori_loop(0, 8, each, 0)

    @pl.when(jnp.logical_not(has_south & has_north))
    def _():
        pltpu.make_async_copy(zero, ext.at[pl.ds(0, HALO)], loc.at[2]).wait()
        pltpu.make_async_copy(zero.at[:, 0], wext.at[pl.ds(0, HALO)], loc.at[3]).wait()


def advect_kernel(dims, ext, wext, out, fields, courant, nat):
    rows, cols, seg, levels = dims
    half = 2 * levels
    r = pl.program_id(0)

    def halo_cells(level, slot, h):
        for n in range(2):
            fields[level, slot, h, n] = pltpu.roll(fields[level, slot, h, seg + n], 1, 0)
            fields[level, slot, h, seg + 2 + n] = pltpu.roll(fields[level, slot, h, 2 + n], 7, 0)

    slot = r % 8
    for h in range(2):
        nat[h] = ext[0, h].astype(F32)
        for j in range(seg):
            fields[0, slot, h, 2 + j] = nat[h, pl.ds(j, 8, stride=seg)]
        halo_cells(0, slot, h)
    nat[2] = wext[0].astype(F32)
    lane = lax.broadcasted_iota(jnp.int32, (8, half), 1)
    wslot = (r + 6) % 8
    for j in range(seg):
        both = 0.5 * nat[2, pl.ds(j, 8, stride=seg)]
        other = pltpu.roll(both, levels, 1)
        courant[wslot, 0, j] = jnp.where(lane < levels, both, other)
        courant[wslot, 1, j] = jnp.where(lane < levels, other, both)

    def part(courant_half, plus, minus, plus2, minus2, f30):
        first = (plus2 - minus2) - 8.0 * (plus - minus)
        second = 16.0 * (plus + minus) - (plus2 + minus2) - f30
        return courant_half * (first + courant_half * second)

    def step(s, c):
        i = r - 2 * s
        here = i % 8
        s2, s1, n1, n2 = ((i + 6) % 8, (i + 7) % 8, (i + 1) % 8, (i + 2) % 8)
        for j in range(seg):
            cu = courant[here, 0, j]
            cv = courant[here, 1, j]
            for h in range(2):
                f = fields[s - 1, here, h, 2 + j]
                f30 = 30.0 * f
                total = part(
                    cu, fields[s - 1, here, h, 3 + j], fields[s - 1, here, h, 1 + j],
                    fields[s - 1, here, h, 4 + j], fields[s - 1, here, h, j], f30,
                ) + part(
                    cv, fields[s - 1, n1, h, 2 + j], fields[s - 1, s1, h, 2 + j],
                    fields[s - 1, n2, h, 2 + j], fields[s - 1, s2, h, 2 + j], f30,
                )
                fields[s, here, h, 2 + j] = f + (1.0 / 6.0) * total
        for h in range(2):
            halo_cells(s, here, h)
        return c

    lax.fori_loop(1, jnp.minimum(r // 4, STEPS) + 1, step, 0)

    @pl.when(r >= 4 * STEPS)
    def _():
        done = r % 8
        for h in range(2):
            for j in range(seg):
                nat[h, pl.ds(j, 8, stride=seg)] = fields[STEPS, done, h, 2 + j]
            out[0, :, h * half : (h + 1) * half] = nat[h, pl.ds(8, cols)].astype(BF16)


def per_device(state, winds, decay, widths):
    rows, cols, chans = state.shape
    levels = winds.shape[2] // 2
    half = 2 * levels
    bands = lax.axis_size("lat")
    pad = cols + 24
    wide_rows = rows + 2 * HALO
    dma = pltpu.SemaphoreType.DMA
    hbm = pl.BlockSpec(memory_space=pl.ANY)
    smem = pl.BlockSpec(memory_space=pltpu.SMEM)
    ext, wext = pl.pallas_call(
        functools.partial(filter_kernel, (bands, rows, cols, pad, levels)),
        out_shape=(
            jax.ShapeDtypeStruct((wide_rows, 2, pad, half), BF16),
            jax.ShapeDtypeStruct((wide_rows, pad, half), BF16),
        ),
        in_specs=[hbm, hbm, smem, smem],
        out_specs=(hbm, hbm),
        scratch_shapes=[
            pltpu.VMEM((rows, cols, chans), F32),
            pltpu.VMEM((rows, 2, cols, half), BF16),
            pltpu.VMEM((2, 2, 4, cols, half), BF16),
            pltpu.VMEM((4, cols, pad), F32),
            pltpu.VMEM((4, 4, cols, pad), F32),
            pltpu.VMEM((4, cols, pad), BF16),
            pltpu.VMEM((4, pad, chans), BF16),
            pltpu.VMEM((4 * cols + 24, half), F32),
            pltpu.VMEM((4, 4, pad, half), BF16),
            pltpu.VMEM((2, pad, half), F32),
            pltpu.VMEM((rows, cols, half), BF16),
            pltpu.VMEM((rows, pad, half), BF16),
            pltpu.VMEM((2, rows, 16, half), BF16),
            pltpu.VMEM((2, rows, 16, half), BF16),
            pltpu.VMEM((rows, 2, pad, half), BF16),
            pltpu.VMEM((2, rows, 2, 16, half), BF16),
            pltpu.VMEM((2, rows, 2, 16, half), BF16),
            pltpu.VMEM((HALO, 2, pad, half), BF16),
            dma((16,)), dma((16, 2)), dma((2, 2, 4)), dma((4, 4)), dma((16, 2)), dma((16, 2)), dma((16, 2)),
            dma((5,)), dma((2,)), dma((2,)), dma((2,)), dma((2,)), dma((4,)),
        ],
        compiler_params=pltpu.CompilerParams(
            collective_id=0, has_side_effects=True, vmem_limit_bytes=56 * 2**20
        ),
        name="filter_and_halo",
    )(state, winds, decay, widths)
    seg = (cols + 2 * HALO) // 8
    return pl.pallas_call(
        functools.partial(advect_kernel, (rows, cols, seg, levels)),
        grid=(wide_rows,),
        out_shape=jax.ShapeDtypeStruct((rows, cols, chans), BF16),
        in_specs=[
            pl.BlockSpec((1, 2, pad, half), lambda r: (r, 0, 0, 0)),
            pl.BlockSpec((1, pad, half), lambda r: (jnp.maximum(r - 2, 0), 0, 0)),
        ],
        out_specs=pl.BlockSpec((1, cols, chans), lambda r: (jnp.maximum(r - 4 * STEPS, 0), 0, 0)),
        scratch_shapes=[
            pltpu.VMEM((STEPS + 1, 8, 2, seg + 4, 8, half), F32),
            pltpu.VMEM((8, 2, seg, 8, half), F32),
            pltpu.VMEM((3, pad, half), F32),
        ],
        compiler_params=pltpu.CompilerParams(vmem_limit_bytes=48 * 2**20),
        name="advect_band",
    )(ext, wext)


def solution(mesh):
    in_specs = (P("lat", "lon", None), P("lat", "lon", None), P(), P())
    out_specs = P("lat", "lon", None)
    return jax.shard_map(
        per_device, mesh=mesh, in_specs=in_specs, out_specs=out_specs, check_vma=False
    )
```

```python
import functools

import jax
import jax.numpy as jnp
from jax import lax
from jax.experimental import pallas as pl
from jax.experimental.pallas import tpu as pltpu
from jax.sharding import PartitionSpec as P

STEPS = 4
HALO = 2 * STEPS
MESH = pl.DeviceIdType.MESH
F32 = jnp.float32
BF16 = jnp.bfloat16
FAR = 1.0e6


def filter_kernel(
    dims, state, winds, decay, widths, ext, wext,
    stf, low, circ, gaps, table, mat, xs, yc, ot, wide, wv, wasm, wedge, wland, easm, eedge, eland, zero,
    ld, fs, fr, rs, rr, hs, hr, wsem, els, elr, wrow_s, wrow_r, loc,
):
    bands, rows, cols, pad, levels = dims
    half = 2 * levels
    lat = lax.axis_index("lat")
    lon = lax.axis_index("lon")
    quarter = bands // 4
    polar = (lat < quarter) | (lat >= bands - quarter)
    twin = jnp.where((lat // quarter) % 2 == 0, lat + quarter, lat - quarter)
    home = jnp.where(polar, lat, twin)
    has_south = lat > 0
    has_north = lat < bands - 1

    def at(la, lo):
        return {"lat": la, "lon": lo}

    def remote(src, dst, send, recv, la, lo):
        return pltpu.make_async_remote_copy(
            src_ref=src, dst_ref=dst, send_sem=send, recv_sem=recv, device_id=at(la, lo), device_id_type=MESH
        )

    barrier = pltpu.get_barrier_semaphore()
    for k in range(4):
        pl.semaphore_signal(barrier, inc=1, device_id=at(twin, (lon + k) % 4), device_id_type=MESH)
        if k:
            pl.semaphore_signal(barrier, inc=1, device_id=at(lat, (lon + k) % 4), device_id_type=MESH)

    for side in (1, bands - 1):
        pl.semaphore_signal(barrier, inc=1, device_id=at((lat + side) % bands, lon), device_id_type=MESH)

    order = []
    for g in range(2):
        for k in (2, 1, 3, 0):
            for part in (1, 0):
                order.append((g, k, part))

    def row_of(g, k, part):
        return 8 * part + 4 * g + (lon + k) % 4

    for g, k, part in order:
        i = row_of(g, k, part)
        pltpu.make_async_copy(state.at[i], stf.at[i], ld.at[i]).start()
    pltpu.make_async_copy(winds, wv, wsem.at[0]).start()

    pl.semaphore_wait(barrier, 9)

    def forward(g, h, k, part, i):
        src = low.at[i, h]
        dst = circ.at[g, h, lon]
        return remote(src, dst, fs.at[i, h], fr.at[g, h, lon], twin if part else lat, (lon + k) % 4)

    @pl.when(polar)
    def _():
        for g in range(2):
            for h in range(2):
                for k in (2, 1, 3, 0):
                    for part in (1, 0):
                        i = row_of(g, k, part)
                        if h == 0:
                            pltpu.make_async_copy(state.at[i], stf.at[i], ld.at[i]).wait()
                            low[i, 0] = stf[i, :, :half].astype(BF16)
                            low[i, 1] = stf[i, :, half:].astype(BF16)
                        if k == 0 and part == 0:
                            pltpu.make_async_copy(low.at[i, h], circ.at[g, h, lon], fr.at[g, h, lon]).start()
                        else:
                            forward(g, h, k, part, i).start()

    pltpu.make_async_copy(winds, wv, wsem.at[0]).wait()
    wedge[0] = wv[:, 0:16, :]
    wedge[1] = wv[:, cols - 16 : cols, :]

    def wind_edge(n):
        return remote(wedge.at[n], wland.at[n], wsem.at[1 + n], wsem.at[3 + n], lat, (lon + (3 if n == 0 else 1)) % 4)

    for n in range(2):
        wind_edge(n).start()

    def state_edge(n):
        return remote(eedge.at[n], eland.at[n], els.at[n], elr.at[n], lat, (lon + (3 if n == 0 else 1)) % 4)

    @pl.when(jnp.logical_not(polar))
    def _():
        def load(i, c):
            pltpu.make_async_copy(state.at[i], stf.at[i], ld.at[i]).wait()
            for h in range(2):
                lanes = slice(h * half, (h + 1) * half)
                eedge[0, i, h] = stf[i, 0:16, lanes].astype(BF16)
                eedge[1, i, h] = stf[i, cols - 16 : cols, lanes].astype(BF16)
            return c

        lax.fori_loop(0, rows, load, 0)
        for n in range(2):
            state_edge(n).start()

    zero[...] = jnp.zeros(zero.shape, BF16)

    @pl.when(jnp.logical_not(has_south))
    def _():
        pltpu.make_async_copy(zero, ext.at[pl.ds(0, HALO)], loc.at[2]).start()
        pltpu.make_async_copy(zero.at[:, 0], wext.at[pl.ds(0, HALO)], loc.at[3]).start()

    @pl.when(jnp.logical_not(has_north))
    def _():
        pltpu.make_async_copy(zero, ext.at[pl.ds(rows + HALO, HALO)], loc.at[2]).start()
        pltpu.make_async_copy(zero.at[:, 0], wext.at[pl.ds(rows + HALO, HALO)], loc.at[3]).start()

    for n in range(2):
        wind_edge(n).wait()

    def assemble(i, c):
        wide[0, 0:8] = wland[1, i, 8:16, :].astype(F32)
        wide[0, pl.ds(8, cols)] = wv[i].astype(F32)
        wide[0, pl.ds(8 + cols, 16)] = wland[0, i].astype(F32)
        wasm[i] = wide[0].astype(BF16)
        return c

    lax.fori_loop(0, rows, assemble, 0)

    def wind_rows(n):
        if n == 0:
            return remote(wasm.at[pl.ds(0, HALO)], wext.at[pl.ds(rows + HALO, HALO)], wrow_s.at[0], wrow_r.at[1], lat - 1, lon)
        return remote(wasm.at[pl.ds(rows - HALO, HALO)], wext.at[pl.ds(0, HALO)], wrow_s.at[1], wrow_r.at[0], lat + 1, lon)

    @pl.when(has_south)
    def _():
        wind_rows(0).start()

    @pl.when(has_north)
    def _():
        wind_rows(1).start()

    wind_local = pltpu.make_async_copy(wasm, wext.at[pl.ds(HALO, rows)], loc.at[0])
    wind_local.start()

    def to_south(src, i, h):
        return remote(src, ext.at[rows + HALO + i, h], hs.at[i, h], hr.at[8 + i, h], lat - 1, lon)

    def to_north(src, i, h):
        return remote(src, ext.at[i - 8, h], hs.at[i, h], hr.at[i - 8, h], lat + 1, lon)

    state_local = pltpu.make_async_copy(easm, ext.at[pl.ds(HALO, rows)], loc.at[1])

    @pl.when(jnp.logical_not(polar))
    def _():
        for n in range(2):
            state_edge(n).wait()

        def assemble_state(i, c):
            for h in range(2):
                lanes = slice(h * half, (h + 1) * half)
                wide[h, 0:8] = eland[1, i, h, 8:16, :].astype(F32)
                wide[h, pl.ds(8, cols)] = stf[i, :, lanes]
                wide[h, pl.ds(8 + cols, 16)] = eland[0, i, h].astype(F32)
                easm[i, h] = wide[h].astype(BF16)
            return c

        lax.fori_loop(0, rows, assemble_state, 0)

        def south(i, c):
            for h in range(2):
                to_south(easm.at[i, h], i, h).start()
            return c

        def north(i, c):
            for h in range(2):
                to_north(easm.at[i, h], i, h).start()
            return c

        lax.fori_loop(0, 8, south, 0)
        lax.fori_loop(8, 16, north, 0)
        state_local.start()

    far = lax.broadcasted_iota(jnp.int32, (cols, pad), 0)
    near = lax.broadcasted_iota(jnp.int32, (cols, pad), 1)
    for d in range(4):
        apart = jnp.abs(far - near - d * cols)
        apart = jnp.minimum(apart, 4 * cols - apart).astype(F32)
        gaps[d] = jnp.where(near < cols, apart, FAR)

    def tabulate(n, c):
        f, d = n // 4, n % 4
        table[f, d] = jnp.exp(-decay[f] * gaps[d])
        return c

    lax.fori_loop(0, 16, tabulate, 0)
    for d in range(4):
        xs[d, pl.ds(pad - 32, 32)] = jnp.zeros((32, 4 * levels), BF16)

    def returned(u, k):
        g, h = u // 2, u % 2
        i = jnp.where(polar, 0, 8) + 4 * g + lon
        t = (lon + k) % 4
        return (
            remote(ot.at[u, t], ext.at[HALO + i, h], rs.at[u, k], rr.at[i, h], home, t),
            pltpu.make_async_copy(ot.at[u, t], ext.at[HALO + i, h], rr.at[i, h]),
        )

    def unit(u, c):
        g, h = u // 2, u % 2
        i = jnp.where(polar, 0, 8) + 4 * g + lon
        reach = widths[home * rows + i].astype(F32)
        for t in range(4):
            pltpu.make_async_copy(low.at[0, 0], circ.at[g, h, t], fr.at[g, h, t]).wait()
        for ff in range(2):
            f = 2 * h + ff
            total = jnp.zeros((1, 1), F32)
            for d in range(4):
                kept = jnp.where(gaps[d, 0:1] <= reach, table[f, d, 0:1], 0.0)
                total = total + jnp.sum(kept, axis=1, keepdims=True)
            scale = 1.0 / total
            for d in range(4):
                mat[d] = jnp.where(gaps[d] <= reach, table[f, d] * scale, 0.0).astype(BF16)
                xs[d, pl.ds(0, cols)] = jnp.concatenate(
                    [circ[g, h, (t + d) % 4, :, ff * levels : (ff + 1) * levels] for t in range(4)], axis=1
                )
            result = jnp.dot(mat[0], xs[0], preferred_element_type=F32)
            for d in range(1, 4):
                result = result + jnp.dot(mat[d], xs[d], preferred_element_type=F32)
            for t in range(4):
                yc[pl.ds(8 + t * cols, cols), ff * levels : (ff + 1) * levels] = result[:, t * levels : (t + 1) * levels]
        yc[0:8] = yc[pl.ds(4 * cols, 8)]
        yc[pl.ds(8 + 4 * cols, 16)] = yc[8:24]
        for t in range(4):
            ot[u, t] = yc[pl.ds(t * cols, pad)].astype(BF16)
        for k in (2, 1, 3):
            returned(u, k)[0].start()

        @pl.when(polar)
        def _():
            returned(u, 0)[1].start()

        @pl.when(jnp.logical_not(polar))
        def _():
            returned(u, 0)[0].start()

        return c

    def pass_on(u):
        g, h = u // 2, u % 2

        @pl.when(polar)
        def _():
            def south(q, c):
                i = 4 * g + q
                pltpu.make_async_copy(ot.at[0, 0], ext.at[HALO + i, h], rr.at[i, h]).wait()

                @pl.when(has_south)
                def _():
                    to_south(ext.at[HALO + i, h], i, h).start()

                return c

            def north(q, c):
                i = 8 + 4 * g + q
                pltpu.make_async_copy(ot.at[0, 0], ext.at[HALO + i, h], rr.at[i, h]).wait()

                @pl.when(has_north)
                def _():
                    to_north(ext.at[HALO + i, h], i, h).start()

                return c

            lax.fori_loop(0, 4, south, 0)
            lax.fori_loop(0, 4, north, 0)

    def stage(n, c):
        @pl.when(n < 4)
        def _():
            unit(n, 0)

        @pl.when(n >= 2)
        def _():
            pass_on(n - 2)

        return c

    lax.fori_loop(0, 6, stage, 0)

    wind_local.wait()

    @pl.when(jnp.logical_not(polar))
    def _():
        state_local.wait()

    @pl.when(polar)
    def _():
        for g in range(2):
            for h in range(2):
                for k in (2, 1, 3, 0):
                    for part in (1, 0):
                        if not (k == 0 and part == 0):
                            forward(g, h, k, part, row_of(g, k, part)).wait_send()

    def sent(u, c):
        for k in (1, 2, 3):
            returned(u, k)[0].wait_send()

        @pl.when(jnp.logical_not(polar))
        def _():
            returned(u, 0)[0].wait_send()

        return c

    lax.fori_loop(0, 4, sent, 0)

    @pl.when(has_south)
    def _():
        wind_rows(0).wait_send()
        wind_rows(1).wait_recv()

        def each(i, c):
            for h in range(2):
                to_south(ext.at[HALO + i, h], i, h).wait_send()
                to_north(ext.at[HALO + i, h], i + 8, h).wait_recv()
            return c

        lax.fori_loop(0, 8, each, 0)

    @pl.when(has_north)
    def _():
        wind_rows(1).wait_send()
        wind_rows(0).wait_recv()

        def each(i, c):
            for h in range(2):
                to_north(ext.at[HALO + i, h], i + 8, h).wait_send()
                to_south(ext.at[HALO + i, h], i, h).wait_recv()
            return c

        lax.fori_loop(0, 8, each, 0)

    @pl.when(jnp.logical_not(has_south & has_north))
    def _():
        pltpu.make_async_copy(zero, ext.at[pl.ds(0, HALO)], loc.at[2]).wait()
        pltpu.make_async_copy(zero.at[:, 0], wext.at[pl.ds(0, HALO)], loc.at[3]).wait()


def advect_kernel(dims, ext, wext, out, f0, f1, f2, f3, f4, weights, nat):
    rows, cols, seg, levels = dims
    half = 2 * levels
    fields = (f0, f1, f2, f3, f4)
    r = pl.program_id(0)

    def halo_cells(field, slot, h):
        for n in range(2):
            field[slot, h, n] = pltpu.roll(field[slot, h, seg + n], 1, 0)
            field[slot, h, seg + 2 + n] = pltpu.roll(field[slot, h, 2 + n], 7, 0)

    slot = r % 8
    for h in range(2):
        nat[h] = ext[0, h].astype(F32)
        for j in range(seg):
            f0[slot, h, 2 + j] = nat[h, pl.ds(j, 8, stride=seg)]
        halo_cells(f0, slot, h)
    nat[2] = wext[0].astype(F32)
    lane = lax.broadcasted_iota(jnp.int32, (8, half), 1)
    wslot = (r + 6) % 8
    for j in range(seg):
        both = nat[2, pl.ds(j, 8, stride=seg)]
        other = pltpu.roll(both, levels, 1)
        square = both * both
        near = (2.0 / 3.0) * both
        near2 = (2.0 / 3.0) * square
        far = (1.0 / 12.0) * both
        far2 = (1.0 / 24.0) * square
        made = (near2 - near, far - far2, near2 + near, -far - far2)
        for n, value in enumerate(made):
            turned = pltpu.roll(value, levels, 1)
            weights[wslot, j, n] = jnp.where(lane < levels, value, turned)
            weights[wslot, j, 4 + n] = jnp.where(lane < levels, turned, value)
        weights[wslot, j, 8] = 1.0 - 1.25 * (square + other * other)

    for s in range(1, STEPS + 1):

        @pl.when(r >= 4 * s)
        def _(s=s):
            old, new = fields[s - 1], fields[s]
            i = r - 2 * s
            here = i % 8
            s2, s1, n1, n2 = ((i + 6) % 8, (i + 7) % 8, (i + 1) % 8, (i + 2) % 8)
            for j in range(seg):
                w = [weights[here, j, n] for n in range(9)]
                for h in range(2):
                    along = (w[0] * old[here, h, 3 + j] + w[1] * old[here, h, 4 + j]) + (
                        w[2] * old[here, h, 1 + j] + w[3] * old[here, h, j]
                    )
                    across = (w[4] * old[n1, h, 2 + j] + w[5] * old[n2, h, 2 + j]) + (
                        w[6] * old[s1, h, 2 + j] + w[7] * old[s2, h, 2 + j]
                    )
                    new[here, h, 2 + j] = w[8] * old[here, h, 2 + j] + (along + across)
            if s < STEPS:
                for h in range(2):
                    halo_cells(new, here, h)

    @pl.when(r >= 4 * STEPS)
    def _():
        done = r % 8
        for h in range(2):
            for j in range(seg):
                nat[h, pl.ds(j, 8, stride=seg)] = f4[done, h, 2 + j]
            out[0, :, h * half : (h + 1) * half] = nat[h, pl.ds(8, cols)].astype(BF16)


def per_device(state, winds, decay, widths):
    rows, cols, chans = state.shape
    levels = winds.shape[2] // 2
    half = 2 * levels
    bands = lax.axis_size("lat")
    pad = cols + 24
    wide_rows = rows + 2 * HALO
    dma = pltpu.SemaphoreType.DMA
    hbm = pl.BlockSpec(memory_space=pl.ANY)
    smem = pl.BlockSpec(memory_space=pltpu.SMEM)
    ext, wext = pl.pallas_call(
        functools.partial(filter_kernel, (bands, rows, cols, pad, levels)),
        out_shape=(
            jax.ShapeDtypeStruct((wide_rows, 2, pad, half), BF16),
            jax.ShapeDtypeStruct((wide_rows, pad, half), BF16),
        ),
        in_specs=[hbm, hbm, smem, smem],
        out_specs=(hbm, hbm),
        scratch_shapes=[
            pltpu.VMEM((rows, cols, chans), F32),
            pltpu.VMEM((rows, 2, cols, half), BF16),
            pltpu.VMEM((2, 2, 4, cols, half), BF16),
            pltpu.VMEM((4, cols, pad), F32),
            pltpu.VMEM((4, 4, cols, pad), F32),
            pltpu.VMEM((4, cols, pad), BF16),
            pltpu.VMEM((4, pad, chans), BF16),
            pltpu.VMEM((4 * cols + 24, half), F32),
            pltpu.VMEM((4, 4, pad, half), BF16),
            pltpu.VMEM((2, pad, half), F32),
            pltpu.VMEM((rows, cols, half), BF16),
            pltpu.VMEM((rows, pad, half), BF16),
            pltpu.VMEM((2, rows, 16, half), BF16),
            pltpu.VMEM((2, rows, 16, half), BF16),
            pltpu.VMEM((rows, 2, pad, half), BF16),
            pltpu.VMEM((2, rows, 2, 16, half), BF16),
            pltpu.VMEM((2, rows, 2, 16, half), BF16),
            pltpu.VMEM((HALO, 2, pad, half), BF16),
            dma((16,)), dma((16, 2)), dma((2, 2, 4)), dma((4, 4)), dma((16, 2)), dma((16, 2)), dma((16, 2)),
            dma((5,)), dma((2,)), dma((2,)), dma((2,)), dma((2,)), dma((4,)),
        ],
        compiler_params=pltpu.CompilerParams(
            collective_id=0, has_side_effects=True, vmem_limit_bytes=56 * 2**20
        ),
        name="filter_and_halo",
    )(state, winds, decay, widths)
    seg = (cols + 2 * HALO) // 8
    return pl.pallas_call(
        functools.partial(advect_kernel, (rows, cols, seg, levels)),
        grid=(wide_rows,),
        out_shape=jax.ShapeDtypeStruct((rows, cols, chans), BF16),
        in_specs=[
            pl.BlockSpec((1, 2, pad, half), lambda r: (r, 0, 0, 0)),
            pl.BlockSpec((1, pad, half), lambda r: (jnp.maximum(r - 2, 0), 0, 0)),
        ],
        out_specs=pl.BlockSpec((1, cols, chans), lambda r: (jnp.maximum(r - 4 * STEPS, 0), 0, 0)),
        scratch_shapes=[
            *[pltpu.VMEM((8, 2, seg + 4, 8, half), F32)] * (STEPS + 1),
            pltpu.VMEM((8, seg, 9, 8, half), F32),
            pltpu.VMEM((3, pad, half), F32),
        ],
        compiler_params=pltpu.CompilerParams(vmem_limit_bytes=48 * 2**20),
        name="advect_band",
    )(ext, wext)


def solution(mesh):
    in_specs = (P("lat", "lon", None), P("lat", "lon", None), P(), P())
    out_specs = P("lat", "lon", None)
    return jax.shard_map(
        per_device, mesh=mesh, in_specs=in_specs, out_specs=out_specs, check_vma=False
    )
```

```python
import functools

import jax
import jax.numpy as jnp
from jax import lax
from jax.experimental import pallas as pl
from jax.experimental.pallas import tpu as pltpu
from jax.sharding import PartitionSpec as P

STEPS = 4
HALO = 2 * STEPS
MESH = pl.DeviceIdType.MESH
F32 = jnp.float32
BF16 = jnp.bfloat16
FAR = 1.0e6
FIELD_ROWS = 6
WEIGHT_ROWS = 7
TURN = (2, 1, 3, 0)


def chunks(count, size):
    return [(a, min(size, count - a)) for a in range(0, count, size)]


def band_kernel(
    dims, state, winds, decay, widths, out,
    stf, low, circ, relay, gaps, table, mat, xs, yc, ot, ext, wext, wv, wide,
    wedge, wland, eedge, eland, f0, f1, f2, f3, weights, nat, ost,
    ld, fs, fr, rl, rls, rs, rr, hs, hr, wsem, esem, wrow, osem,
):
    bands, rows, cols, pad, levels, seg = dims
    half = 2 * levels
    lat = lax.axis_index("lat")
    lon = lax.axis_index("lon")
    quarter = bands // 4
    polar = (lat < quarter) | (lat >= bands - quarter)
    inner = jnp.logical_not(polar)
    twin = jnp.where((lat // quarter) % 2 == 0, lat + quarter, lat - quarter)
    home = jnp.where(polar, lat, twin)
    odd = lat % 2
    home_odd = home % 2
    first = lat - 1 + 2 * odd
    last = lat + 1 - 2 * odd
    has_first = (first >= 0) & (first < bands)

    def at(la, lo):
        return {"lat": la, "lon": lo}

    def actual(p, flip):
        return jnp.where(flip == 1, rows - 1 - p, p)

    def remote(src, dst, send, recv, la, lo):
        return pltpu.make_async_remote_copy(
            src_ref=src, dst_ref=dst, send_sem=send, recv_sem=recv, device_id=at(la, lo), device_id_type=MESH
        )

    barrier = pltpu.get_barrier_semaphore()
    for k in range(4):
        pl.semaphore_signal(barrier, inc=1, device_id=at(twin, (lon + k) % 4), device_id_type=MESH)
        if k:
            pl.semaphore_signal(barrier, inc=1, device_id=at(lat, (lon + k) % 4), device_id_type=MESH)
    for side in (1, bands - 1):
        pl.semaphore_signal(barrier, inc=1, device_id=at((lat + side) % bands, lon), device_id_type=MESH)

    def nth_row(n):
        q, place = n // 4, n % 4
        k = jnp.where(place == 0, 2, jnp.where(place == 1, 1, jnp.where(place == 2, 3, 0)))
        return actual(4 * q + (lon + k) % 4, odd)

    def load(n):
        return pltpu.make_async_copy(state.at[nth_row(n)], stf.at[n % 4], ld.at[n % 4])

    for n in range(4):
        load(n).start()
    wind_load = pltpu.make_async_copy(winds, wv, wsem.at[0])
    wind_load.start()

    pl.semaphore_wait(barrier, 9)

    def convert(n, c):
        load(n).wait()
        i = nth_row(n)
        for h in range(2):
            lanes = slice(h * half, (h + 1) * half)
            low[i, h] = stf[n % 4, :, lanes].astype(BF16)
            eedge[0, i, h] = stf[n % 4, 0:16, lanes].astype(BF16)
            eedge[1, i, h] = stf[n % 4, cols - 16 : cols, lanes].astype(BF16)

        @pl.when(n + 4 < rows)
        def _():
            load(n + 4).start()

        return c

    def own_slot(n):
        return n - 3 if n >= 6 else (n - 1) // 2

    def shared(n):
        return n in (0, 2, 4)

    def forward(n, k):
        q, h = n // 2, n % 2
        target = (lon + k) % 4
        src = low.at[actual(4 * q + target, odd), h]
        if shared(n):
            return remote(src, relay.at[n // 2, target], fs.at[n, k], rl.at[n // 2, target], twin, lon)
        if k == 0:
            return pltpu.make_async_copy(src, circ.at[own_slot(n), lon], fr.at[own_slot(n), lon])
        return remote(src, circ.at[own_slot(n), lon], fs.at[n, k], fr.at[own_slot(n), lon], lat, target)

    def send_group(q):
        lax.fori_loop(4 * q, 4 * q + 4, convert, 0)

        @pl.when(polar)
        def _():
            for n in (2 * q, 2 * q + 1):
                for k in TURN:
                    forward(n, k).start()

    send_group(0)
    send_group(1)

    wind_load.wait()
    wedge[0] = wv[:, 0:16, :]
    wedge[1] = wv[:, cols - 16 : cols, :]

    def beside(n):
        return (lon + (3 if n == 0 else 1)) % 4

    def wind_edge(n):
        return remote(wedge.at[n], wland.at[n], wsem.at[1 + n], wsem.at[3 + n], lat, beside(n))

    def state_edge(n):
        return remote(eedge.at[n], eland.at[n], esem.at[n], esem.at[2 + n], lat, beside(n))

    for n in range(2):
        wind_edge(n).start()

    send_group(2)
    send_group(3)

    @pl.when(inner)
    def _():
        for n in range(2):
            state_edge(n).start()

    @pl.when(jnp.logical_not(has_first))
    def _():
        ext[0:HALO] = jnp.zeros((HALO, 2, seg, 8, half), BF16)
        wext[0:HALO] = jnp.zeros((HALO, seg, 8, half), BF16)

    def wind_row(i, c):
        wide[0, 0:8] = wland[1, i, 8:16, :].astype(F32)
        wide[0, pl.ds(8, cols)] = wv[i].astype(F32)
        wide[0, pl.ds(8 + cols, 16)] = wland[0, i].astype(F32)
        e = HALO + actual(i, odd)
        for j in range(seg):
            wext[e, j] = wide[0, pl.ds(j, 8, stride=seg)].astype(BF16)
        return c

    for n in range(2):
        wind_edge(n).wait()
    lax.fori_loop(0, rows, wind_row, 0)

    def wind_first(p):
        return remote(wext.at[HALO + p], wext.at[7 - p], wrow.at[0], wrow.at[1], first, lon)

    def wind_last(p):
        return remote(wext.at[HALO + p], wext.at[39 - p], wrow.at[2], wrow.at[3], last, lon)

    def all_wind_first():
        return remote(wext.at[pl.ds(8, 8)], wext.at[pl.ds(0, 8)], wrow.at[0], wrow.at[1], first, lon)

    def all_wind_last():
        return remote(wext.at[pl.ds(16, 8)], wext.at[pl.ds(24, 8)], wrow.at[2], wrow.at[3], last, lon)

    @pl.when(has_first)
    def _():
        for p in range(8):
            wind_first(p).start()

    for p in range(8, 16):
        wind_last(p).start()

    def to_first(p):
        return remote(ext.at[HALO + p], ext.at[7 - p], hs.at[p], hr.at[7 - p], first, lon)

    def to_last(p):
        return remote(ext.at[HALO + p], ext.at[39 - p], hs.at[p], hr.at[23 - p], last, lon)

    @pl.when(inner)
    def _():
        for n in range(2):
            state_edge(n).wait()

        def state_row(i, c):
            e = HALO + actual(i, odd)
            for h in range(2):
                wide[h, 0:8] = eland[1, i, h, 8:16, :].astype(F32)
                wide[h, pl.ds(8, cols)] = low[i, h].astype(F32)
                wide[h, pl.ds(8 + cols, 16)] = eland[0, i, h].astype(F32)
                for j in range(seg):
                    ext[e, h, j] = wide[h, pl.ds(j, 8, stride=seg)].astype(BF16)
            return c

        lax.fori_loop(0, rows, state_row, 0)

        def give(p, c):
            to_first(p).start()
            to_last(p + 8).start()
            return c

        lax.fori_loop(0, 8, give, 0)

    there = lax.broadcasted_iota(jnp.int32, (cols, pad), 0)
    here_ = lax.broadcasted_iota(jnp.int32, (cols, pad), 1)
    for d in range(4):
        apart = jnp.abs(there - here_ - d * cols)
        apart = jnp.minimum(apart, 4 * cols - apart).astype(F32)
        gaps[d] = jnp.where(here_ < cols, apart, FAR)

    def tabulate(n, c):
        f, d = n // 4, n % 4
        table[f, d] = jnp.exp(-decay[f] * gaps[d]).astype(BF16)
        return c

    lax.fori_loop(0, 16, tabulate, 0)
    for d in range(4):
        xs[d, pl.ds(pad - 32, 32)] = jnp.zeros((32, 4 * levels), BF16)

    def relay_copy(m, k):
        target = (lon + k) % 4
        if k == 0:
            return pltpu.make_async_copy(relay.at[m, target], circ.at[m, lon], fr.at[m, lon])
        return remote(relay.at[m, target], circ.at[m, lon], rls.at[m, k], fr.at[m, lon], lat, target)

    def pass_relay(m):
        for k in TURN:
            target = (lon + k) % 4
            pltpu.make_async_copy(low.at[0, 0], relay.at[m, target], rl.at[m, target]).wait()
            relay_copy(m, k).start()

    def placed(n):
        slot = jnp.where(n >= 6, n - 3, (n - 1) // 2)
        return slot, n // 2, jnp.where(polar, n % 2, 0)

    def returned(n, k):
        slot, q, h = placed(n)
        p = 4 * q + lon
        return remote(
            ot.at[slot, (lon + k) % 4], ext.at[HALO + p, h], rs.at[slot, k], rr.at[p, h], home, (lon + k) % 4
        )

    def filter_unit(n):
        slot, q, h = placed(n)
        i = actual(4 * q + lon, home_odd)
        reach = widths[home * rows + i].astype(F32)
        for t in range(4):
            pltpu.make_async_copy(low.at[0, 0], circ.at[slot, t], fr.at[slot, t]).wait()
        for ff in range(2):
            f = 2 * h + ff
            rate = decay[f]
            total = jnp.zeros((1, 1), F32)
            for d in range(4):
                gap = gaps[d, 0:1]
                kept = jnp.where(gap <= reach, jnp.exp(-rate * gap), 0.0)
                total = total + jnp.sum(kept, axis=1, keepdims=True)
            scale = 1.0 / total
            for d in range(4):
                mat[d] = jnp.where(gaps[d] <= reach, table[f, d].astype(F32), 0.0).astype(BF16)
                xs[d, pl.ds(0, cols)] = jnp.concatenate(
                    [circ[slot, (t + d) % 4, :, ff * levels : (ff + 1) * levels] for t in range(4)], axis=1
                )
            result = jnp.dot(mat[0], xs[0], preferred_element_type=F32)
            for d in range(1, 4):
                result = result + jnp.dot(mat[d], xs[d], preferred_element_type=F32)
            result = result * scale
            for t in range(4):
                yc[pl.ds(8 + t * cols, cols), ff * levels : (ff + 1) * levels] = result[:, t * levels : (t + 1) * levels]
        yc[0:8] = yc[pl.ds(4 * cols, 8)]
        yc[pl.ds(8 + 4 * cols, 16)] = yc[8:24]
        for t in range(4):
            for j in range(seg):
                ot[slot, t, j] = yc[pl.ds(t * cols + j, 8, stride=seg)].astype(BF16)
        for k in (2, 1, 3):
            returned(n, k).start()

        @pl.when(polar)
        def _():
            pltpu.make_async_copy(ot.at[slot, lon], ext.at[HALO + 4 * q + lon, h], rr.at[4 * q + lon, h]).start()

        @pl.when(inner)
        def _():
            returned(n, 0).start()

    def pass_on(q):
        def each(p, c):
            for h in range(2):
                pltpu.make_async_copy(ot.at[0, 0], ext.at[HALO + p, h], rr.at[p, h]).wait()

            @pl.when((p < 8) & has_first)
            def _():
                to_first(p).start()

            @pl.when(p >= 8)
            def _():
                to_last(p).start()

            return c

        lax.fori_loop(4 * q, 4 * q + 4, each, 0)

    fields = (f0, f1, f2, f3)
    upward = 1.0 - 2.0 * odd.astype(F32)

    def halo_cells(field, slot, h):
        for n in range(2):
            field[slot, h, n] = pltpu.roll(field[slot, h, seg + n], 1, 0)
            field[slot, h, seg + 2 + n] = pltpu.roll(field[slot, h, 2 + n], 7, 0)

    def written(p):
        return pltpu.make_async_copy(ost.at[p % 4], out.at[actual(p, odd)], osem.at[p % 4])

    def advance(r, c):
        slot = lax.rem(r, FIELD_ROWS)
        for h in range(2):
            for a, n in chunks(seg, 8):
                f0[slot, h, pl.ds(2 + a, n)] = ext[r, h, pl.ds(a, n)].astype(F32)
            halo_cells(f0, slot, h)

        @pl.when(r >= 4)
        def _():
            made = lax.rem(r - 2, WEIGHT_ROWS)
            for a, n in chunks(seg, 8):
                both = wext[r - 2, pl.ds(a, n)].astype(F32)
                lane = lax.broadcasted_iota(jnp.int32, (n, 8, half), 2)
                other = pltpu.roll(both, levels, 2)
                cu = jnp.where(lane < levels, both, other)
                cv = jnp.where(lane < levels, other, both)
                pairs = ((cu, cu * cu), (cv * upward, cv * cv))
                for m, (one, square) in enumerate(pairs):
                    near, near2 = (2.0 / 3.0) * one, (2.0 / 3.0) * square
                    far, far2 = (1.0 / 12.0) * one, (1.0 / 24.0) * square
                    for w, value in enumerate((near2 - near, far - far2, near2 + near, -far - far2)):
                        weights[made, 4 * m + w, pl.ds(a, n)] = value
                weights[made, 8, pl.ds(a, n)] = 1.0 - 1.25 * (pairs[0][1] + pairs[1][1])

        for s in range(1, STEPS + 1):

            @pl.when(r >= 4 * s)
            def _(s=s):
                old = fields[s - 1]
                i = r - 2 * s
                wrow_ = lax.rem(i, WEIGHT_ROWS)
                here, ahead, ahead2 = (lax.rem(i + o, FIELD_ROWS) for o in (0, 1, 2))
                behind2, behind = (lax.rem(i + o, FIELD_ROWS) for o in (4, 5))
                for a, n in chunks(seg, 4):
                    w = [weights[wrow_, m, pl.ds(a, n)] for m in range(9)]
                    for h in range(2):

                        def cell(row, shift):
                            return old[row, h, pl.ds(2 + a + shift, n)]

                        along = (w[0] * cell(here, 1) + w[1] * cell(here, 2)) + (
                            w[2] * cell(here, -1) + w[3] * cell(here, -2)
                        )
                        across = (w[4] * cell(ahead, 0) + w[5] * cell(ahead2, 0)) + (
                            w[6] * cell(behind, 0) + w[7] * cell(behind2, 0)
                        )
                        value = w[8] * cell(here, 0) + (along + across)
                        if s < STEPS:
                            fields[s][here, h, pl.ds(2 + a, n)] = value
                        else:
                            for m in range(n):
                                nat[h, pl.ds(a + m, 8, stride=seg)] = value[m]
                if s < STEPS:
                    for h in range(2):
                        halo_cells(fields[s], here, h)
                else:
                    p = r - 16

                    @pl.when(p >= 4)
                    def _():
                        written(p - 4).wait()

                    for h in range(2):
                        ost[p % 4, :, h * half : (h + 1) * half] = nat[h, pl.ds(8, cols)].astype(BF16)
                    written(p).start()

        return c

    def stage(n, c):
        for m in range(3):

            @pl.when(inner & (n == 2 * m))
            def _(m=m):
                pass_relay(m)

        @pl.when(((n % 2 == 1) & (n <= 5)) | (polar & ((n == 6) | (n == 7))))
        def _():
            filter_unit(n)

        @pl.when(polar & ((n == 3) | (n == 5) | (n == 7) | (n == 8)))
        def _():
            pass_on(jnp.where(n == 8, 3, (n - 3) // 2))

        @pl.when(n == 6)
        def _():
            all_wind_last().wait()

            @pl.when(has_first)
            def _():
                all_wind_first().wait()
                for e in range(8):
                    to_first(7 - e).wait_recv()

        @pl.when(n == 8)
        def _():
            for e in range(8, 16):
                to_last(23 - e).wait_recv()

        begin = jnp.where(n == 8, 20, jnp.where(n == 7, 6, 0))
        end = jnp.where(n == 8, 32, jnp.where(n == 7, 20, jnp.where(n == 6, 6, 0)))
        lax.fori_loop(begin, end, advance, 0)
        return c

    lax.fori_loop(0, 9, stage, 0)

    for p in range(12, 16):
        written(p).wait()

    @pl.when(polar)
    def _():
        for n in range(8):
            for k in TURN:
                if k or shared(n):
                    forward(n, k).wait_send()

    @pl.when(inner)
    def _():
        for m in range(3):
            for k in (1, 2, 3):
                relay_copy(m, k).wait_send()

    for n in (1, 3, 5, 6, 7):

        @pl.when(polar if n > 5 else n > 0)
        def _(n=n):
            for k in (1, 2, 3):
                returned(n, k).wait_send()

            @pl.when(inner)
            def _():
                returned(n, 0).wait_send()

    for p in range(8, 16):
        to_last(p).wait_send()

    @pl.when(has_first)
    def _():
        for p in range(8):
            to_first(p).wait_send()


def per_device(state, winds, decay, widths):
    rows, cols, chans = state.shape
    levels = winds.shape[2] // 2
    half = 2 * levels
    bands = lax.axis_size("lat")
    pad = cols + 24
    seg = (cols + 2 * HALO) // 8
    deep = rows + 2 * HALO
    dma = pltpu.SemaphoreType.DMA
    vm = pltpu.VMEM
    hbm = pl.BlockSpec(memory_space=pl.ANY)
    smem = pl.BlockSpec(memory_space=pltpu.SMEM)
    return pl.pallas_call(
        functools.partial(band_kernel, (bands, rows, cols, pad, levels, seg)),
        out_shape=jax.ShapeDtypeStruct((rows, cols, chans), BF16),
        in_specs=[hbm, hbm, smem, smem],
        out_specs=hbm,
        scratch_shapes=[
            vm((4, cols, chans), F32),
            vm((rows, 2, cols, half), BF16),
            vm((5, 4, cols, half), BF16),
            vm((3, 4, cols, half), BF16),
            vm((4, cols, pad), F32),
            vm((4, 4, cols, pad), BF16),
            vm((4, cols, pad), BF16),
            vm((4, pad, chans), BF16),
            vm((4 * cols + 24, half), F32),
            vm((5, 4, seg, 8, half), BF16),
            vm((deep, 2, seg, 8, half), BF16),
            vm((deep, seg, 8, half), BF16),
            vm((rows, cols, half), BF16),
            vm((2, pad, half), F32),
            vm((2, rows, 16, half), BF16),
            vm((2, rows, 16, half), BF16),
            vm((2, rows, 2, 16, half), BF16),
            vm((2, rows, 2, 16, half), BF16),
            *[vm((FIELD_ROWS, 2, seg + 4, 8, half), F32)] * STEPS,
            vm((WEIGHT_ROWS, 9, seg, 8, half), F32),
            vm((2, pad, half), F32),
            vm((4, cols, chans), BF16),
            dma((4,)), dma((8, 4)), dma((5, 4)), dma((3, 4)), dma((3, 4)), dma((5, 4)), dma((16, 2)),
            dma((16,)), dma((16,)), dma((5,)), dma((4,)), dma((4,)), dma((4,)),
        ],
        compiler_params=pltpu.CompilerParams(
            collective_id=0, has_side_effects=True, vmem_limit_bytes=60 * 2**20
        ),
        name="filter_and_advect",
    )(state, winds, decay, widths)


def solution(mesh):
    in_specs = (P("lat", "lon", None), P("lat", "lon", None), P(), P())
    out_specs = P("lat", "lon", None)
    return jax.shard_map(
        per_device, mesh=mesh, in_specs=in_specs, out_specs=out_specs, check_vma=False
    )
```

```python
import functools

import jax
import jax.numpy as jnp
from jax import lax
from jax.experimental import pallas as pl
from jax.experimental.pallas import tpu as pltpu
from jax.sharding import PartitionSpec as P

STEPS = 4
HALO = 2 * STEPS
MESH = pl.DeviceIdType.MESH
F32 = jnp.float32
BF16 = jnp.bfloat16
FAR = 1.0e6
FIELD_ROWS = 6
WEIGHT_ROWS = 7
TURN = (2, 1, 3, 0)
SHARED = 3
SHARED_EDGE = 1
SWEEP = ((8, 0, 8), (9, 8, 14), (10, 14, 20), (11, 20, 32))
LOADS = 8


def chunks(count, size):
    return [(a, min(size, count - a)) for a in range(0, count, size)]


def band_kernel(
    dims, state, winds, decay, widths, out,
    stf, low, circ, relay, gaps, table, mat, xs, yc, ot, ext, wext, wv, wide,
    wedge, wland, eedge, eland, f0, f1, f2, f3, weights, nat, ost,
    ld, fs, fr, rl, rls, rs, rr, hs, hr, wsem, esem, wrow, osem,
):
    bands, rows, cols, pad, levels, seg = dims
    half = 2 * levels
    lat = lax.axis_index("lat")
    lon = lax.axis_index("lon")
    quarter = bands // 4
    polar = (lat < quarter) | (lat >= bands - quarter)
    inner = jnp.logical_not(polar)
    twin = jnp.where((lat // quarter) % 2 == 0, lat + quarter, lat - quarter)
    home = jnp.where(polar, lat, twin)
    edge = (home // 2 == quarter // 2 - 1) | (home // 2 == (bands - quarter) // 2)
    parts = jnp.where(edge, SHARED_EDGE, SHARED)
    down = (lat + 1) % 2
    home_down = (home + 1) % 2
    first = lat - 1 + 2 * down
    last = lat + 1 - 2 * down
    has_last = (last >= 0) & (last < bands)

    def at(la, lo):
        return {"lat": la, "lon": lo}

    def actual(p, flip):
        return jnp.where(flip == 1, rows - 1 - p, p)

    def remote(src, dst, send, recv, la, lo):
        return pltpu.make_async_remote_copy(
            src_ref=src, dst_ref=dst, send_sem=send, recv_sem=recv, device_id=at(la, lo), device_id_type=MESH
        )

    barrier = pltpu.get_barrier_semaphore()
    for k in range(4):
        pl.semaphore_signal(barrier, inc=1, device_id=at(twin, (lon + k) % 4), device_id_type=MESH)
        if k:
            pl.semaphore_signal(barrier, inc=1, device_id=at(lat, (lon + k) % 4), device_id_type=MESH)
    for side in (1, bands - 1):
        pl.semaphore_signal(barrier, inc=1, device_id=at((lat + side) % bands, lon), device_id_type=MESH)

    def nth_row(n):
        q, place = n // 4, n % 4
        k = jnp.where(place == 0, 2, jnp.where(place == 1, 1, jnp.where(place == 2, 3, 0)))
        return actual(4 * q + (lon + k) % 4, down)

    def load(n):
        return pltpu.make_async_copy(state.at[nth_row(n)], stf.at[n % LOADS], ld.at[n % LOADS])

    for n in range(LOADS):
        load(n).start()
    wind_load = pltpu.make_async_copy(winds, wv, wsem.at[0])
    wind_load.start()

    pl.semaphore_wait(barrier, 9)

    def convert(n, c):
        load(n).wait()
        i = nth_row(n)
        for h in range(2):
            lanes = slice(h * half, (h + 1) * half)
            low[i, h] = stf[n % LOADS, :, lanes].astype(BF16)
            eedge[0, i, h] = stf[n % LOADS, 0:16, lanes].astype(BF16)
            eedge[1, i, h] = stf[n % LOADS, cols - 16 : cols, lanes].astype(BF16)

        @pl.when(n + LOADS < rows)
        def _():
            load(n + LOADS).start()

        return c

    def own_slot(n):
        return n - jnp.minimum(parts, (n + 1) // 2)

    def shared(n):
        return parts > n // 2 if n % 2 == 0 else lat < 0

    def forward(n, k):
        q, h = n // 2, n % 2
        target = (lon + k) % 4
        src = low.at[actual(4 * q + target, down), h]
        slot = own_slot(n)
        if k == 0:
            own = pltpu.make_async_copy(src, circ.at[slot, lon], fr.at[slot, lon])
        else:
            own = remote(src, circ.at[slot, lon], fs.at[n, k], fr.at[slot, lon], lat, target)
        if n % 2:
            return own, None
        return own, remote(src, relay.at[n // 2, target], fs.at[n, k], rl.at[n // 2, target], twin, lon)

    def send_group(q):
        for n in (2 * q, 2 * q + 1):

            @pl.when(jnp.logical_not(shared(n)))
            def _(n=n):
                for k in TURN:
                    forward(n, k)[0].start()

            if n % 2 == 0:

                @pl.when(shared(n))
                def _(n=n):
                    for k in TURN:
                        forward(n, k)[1].start()

    for q in range(2):
        lax.fori_loop(4 * q, 4 * q + 4, convert, 0)

        @pl.when(polar)
        def _(q=q):
            send_group(q)

    wind_load.wait()
    wedge[0] = wv[:, 0:16, :]
    wedge[1] = wv[:, cols - 16 : cols, :]

    def beside(n):
        return (lon + (3 if n == 0 else 1)) % 4

    def wind_edge(n):
        return remote(wedge.at[n], wland.at[n], wsem.at[1 + n], wsem.at[3 + n], lat, beside(n))

    def state_edge(n):
        return remote(eedge.at[n], eland.at[n], esem.at[n], esem.at[2 + n], lat, beside(n))

    for n in range(2):
        wind_edge(n).start()

    lax.fori_loop(8, 16, convert, 0)

    @pl.when(inner)
    def _():
        for n in range(2):
            state_edge(n).start()

    there = lax.broadcasted_iota(jnp.int32, (cols, pad), 0)
    here_ = lax.broadcasted_iota(jnp.int32, (cols, pad), 1)
    for d in range(4):
        apart = jnp.abs(there - here_ - d * cols)
        apart = jnp.minimum(apart, 4 * cols - apart).astype(F32)
        gaps[d] = jnp.where(here_ < cols, apart, FAR)

    def tabulate(n, c):
        f, d = n // 4, n % 4
        table[f, d] = jnp.exp(-decay[f] * gaps[d]).astype(BF16)
        return c

    lax.fori_loop(0, 16, tabulate, 0)
    for d in range(4):
        xs[d, pl.ds(pad - 32, 32)] = jnp.zeros((32, 4 * levels), BF16)

    @pl.when(polar)
    def _():
        send_group(2)

    @pl.when(jnp.logical_not(has_last))
    def _():
        ext[rows + HALO : rows + 2 * HALO] = jnp.zeros((HALO, 2, seg, 8, half), BF16)
        wext[rows + HALO : rows + 2 * HALO] = jnp.zeros((HALO, seg, 8, half), BF16)

    def wind_row(i, c):
        wide[0, 0:8] = wland[1, i, 8:16, :].astype(F32)
        wide[0, pl.ds(8, cols)] = wv[i].astype(F32)
        wide[0, pl.ds(8 + cols, 16)] = wland[0, i].astype(F32)
        e = HALO + actual(i, down)
        for j in range(seg):
            wext[e, j] = wide[0, pl.ds(j, 8, stride=seg)].astype(BF16)
        return c

    def wind_first(p):
        return remote(wext.at[HALO + p], wext.at[7 - p], wrow.at[0], wrow.at[1], first, lon)

    def wind_last(p):
        return remote(wext.at[HALO + p], wext.at[39 - p], wrow.at[2], wrow.at[3], last, lon)

    def all_wind_first():
        return remote(wext.at[pl.ds(8, 8)], wext.at[pl.ds(0, 8)], wrow.at[0], wrow.at[1], first, lon)

    def all_wind_last():
        return remote(wext.at[pl.ds(16, 8)], wext.at[pl.ds(24, 8)], wrow.at[2], wrow.at[3], last, lon)

    def to_first(p):
        return remote(ext.at[HALO + p], ext.at[7 - p], hs.at[p], hr.at[7 - p], first, lon)

    def to_last(p):
        return remote(ext.at[HALO + p], ext.at[39 - p], hs.at[p], hr.at[23 - p], last, lon)

    @pl.when(inner)
    def _():
        for n in range(2):
            state_edge(n).wait()

        def state_row(i, c):
            e = HALO + actual(i, down)
            for h in range(2):
                wide[h, 0:8] = eland[1, i, h, 8:16, :].astype(F32)
                wide[h, pl.ds(8, cols)] = low[i, h].astype(F32)
                wide[h, pl.ds(8 + cols, 16)] = eland[0, i, h].astype(F32)
                for j in range(seg):
                    ext[e, h, j] = wide[h, pl.ds(j, 8, stride=seg)].astype(BF16)
            return c

        lax.fori_loop(0, rows, state_row, 0)

        def give(p, c):
            to_first(p).start()
            return c

        lax.fori_loop(0, 8, give, 0)

    def spread_winds():
        for n in range(2):
            wind_edge(n).wait()
        lax.fori_loop(0, rows, wind_row, 0)

        for p in range(8):
            wind_first(p).start()

        @pl.when(has_last)
        def _():
            for p in range(8, 16):
                wind_last(p).start()

    def relay_copy(m, k):
        target = (lon + k) % 4
        if k == 0:
            return pltpu.make_async_copy(relay.at[m, target], circ.at[m, lon], fr.at[m, lon])
        return remote(relay.at[m, target], circ.at[m, lon], rls.at[m, k], fr.at[m, lon], lat, target)

    def pass_relay(m):
        for k in TURN:
            target = (lon + k) % 4
            pltpu.make_async_copy(low.at[0, 0], relay.at[m, target], rl.at[m, target]).wait()
            relay_copy(m, k).start()

    def placed(n):
        slot = jnp.where(polar, n - jnp.minimum(parts, (n + 1) // 2), (n - 1) // 2)
        return slot, n // 2, jnp.where(polar, n % 2, 0)

    def returned(n, k):
        slot, q, h = placed(n)
        p = 4 * q + lon
        return remote(
            ot.at[slot, (lon + k) % 4], ext.at[HALO + p, h], rs.at[slot, k], rr.at[p, h], home, (lon + k) % 4
        )

    def filter_unit(n):
        slot, q, h = placed(n)
        i = actual(4 * q + lon, home_down)
        reach = widths[home * rows + i].astype(F32)
        for t in range(4):
            pltpu.make_async_copy(low.at[0, 0], circ.at[slot, t], fr.at[slot, t]).wait()
        for ff in range(2):
            f = 2 * h + ff
            rate = decay[f]
            total = jnp.zeros((1, 1), F32)
            for d in range(4):
                gap = gaps[d, 0:1]
                kept = jnp.where(gap <= reach, jnp.exp(-rate * gap), 0.0)
                total = total + jnp.sum(kept, axis=1, keepdims=True)
            scale = 1.0 / total
            for d in range(4):
                mat[d] = jnp.where(gaps[d] <= reach, table[f, d].astype(F32), 0.0).astype(BF16)
                xs[d, pl.ds(0, cols)] = jnp.concatenate(
                    [circ[slot, (t + d) % 4, :, ff * levels : (ff + 1) * levels] for t in range(4)], axis=1
                )
            result = jnp.dot(mat[0], xs[0], preferred_element_type=F32)
            for d in range(1, 4):
                result = result + jnp.dot(mat[d], xs[d], preferred_element_type=F32)
            result = result * scale
            for t in range(4):
                yc[pl.ds(8 + t * cols, cols), ff * levels : (ff + 1) * levels] = result[:, t * levels : (t + 1) * levels]
        yc[0:8] = yc[pl.ds(4 * cols, 8)]
        yc[pl.ds(8 + 4 * cols, 16)] = yc[8:24]
        for t in range(4):
            for j in range(seg):
                ot[slot, t, j] = yc[pl.ds(t * cols + j, 8, stride=seg)].astype(BF16)
        for k in (2, 1, 3):
            returned(n, k).start()

        @pl.when(polar)
        def _():
            pltpu.make_async_copy(ot.at[slot, lon], ext.at[HALO + 4 * q + lon, h], rr.at[4 * q + lon, h]).start()

        @pl.when(inner)
        def _():
            returned(n, 0).start()

    def pass_on(q):
        def each(p, c):
            for h in range(2):
                pltpu.make_async_copy(ot.at[0, 0], ext.at[HALO + p, h], rr.at[p, h]).wait()

            @pl.when(p < 8)
            def _():
                to_first(p).start()

            @pl.when((p >= 8) & has_last)
            def _():
                to_last(p).start()

            return c

        lax.fori_loop(4 * q, 4 * q + 4, each, 0)

    fields = (f0, f1, f2, f3)
    upward = 1.0 - 2.0 * down.astype(F32)

    def halo_cells(field, slot, h):
        for n in range(2):
            field[slot, h, n] = pltpu.roll(field[slot, h, seg + n], 1, 0)
            field[slot, h, seg + 2 + n] = pltpu.roll(field[slot, h, 2 + n], 7, 0)

    def written(p):
        return pltpu.make_async_copy(ost.at[p % 4], out.at[actual(p, down)], osem.at[p % 4])

    def advance(r, c):
        slot = lax.rem(r, FIELD_ROWS)
        for h in range(2):
            for a, n in chunks(seg, 8):
                f0[slot, h, pl.ds(2 + a, n)] = ext[r, h, pl.ds(a, n)].astype(F32)
            halo_cells(f0, slot, h)

        @pl.when(r >= 4)
        def _():
            made = lax.rem(r - 2, WEIGHT_ROWS)
            for a, n in chunks(seg, 8):
                both = wext[r - 2, pl.ds(a, n)].astype(F32)
                lane = lax.broadcasted_iota(jnp.int32, (n, 8, half), 2)
                other = pltpu.roll(both, levels, 2)
                cu = jnp.where(lane < levels, both, other)
                cv = jnp.where(lane < levels, other, both)
                pairs = ((cu, cu * cu), (cv * upward, cv * cv))
                for m, (one, square) in enumerate(pairs):
                    near, near2 = (2.0 / 3.0) * one, (2.0 / 3.0) * square
                    far, far2 = (1.0 / 12.0) * one, (1.0 / 24.0) * square
                    for w, value in enumerate((near2 - near, far - far2, near2 + near, -far - far2)):
                        weights[made, 4 * m + w, pl.ds(a, n)] = value
                weights[made, 8, pl.ds(a, n)] = 1.0 - 1.25 * (pairs[0][1] + pairs[1][1])

        for s in range(1, STEPS + 1):

            @pl.when(r >= 4 * s)
            def _(s=s):
                old = fields[s - 1]
                i = r - 2 * s
                wrow_ = lax.rem(i, WEIGHT_ROWS)
                here, ahead, ahead2 = (lax.rem(i + o, FIELD_ROWS) for o in (0, 1, 2))
                behind2, behind = (lax.rem(i + o, FIELD_ROWS) for o in (4, 5))
                for a, n in chunks(seg, 4):
                    w = [weights[wrow_, m, pl.ds(a, n)] for m in range(9)]
                    for h in range(2):

                        def cell(row, shift):
                            return old[row, h, pl.ds(2 + a + shift, n)]

                        along = (w[0] * cell(here, 1) + w[1] * cell(here, 2)) + (
                            w[2] * cell(here, -1) + w[3] * cell(here, -2)
                        )
                        across = (w[4] * cell(ahead, 0) + w[5] * cell(ahead2, 0)) + (
                            w[6] * cell(behind, 0) + w[7] * cell(behind2, 0)
                        )
                        value = w[8] * cell(here, 0) + (along + across)
                        if s < STEPS:
                            fields[s][here, h, pl.ds(2 + a, n)] = value
                        else:
                            for m in range(n):
                                nat[h, pl.ds(a + m, 8, stride=seg)] = value[m]
                if s < STEPS:
                    for h in range(2):
                        halo_cells(fields[s], here, h)
                else:
                    p = r - 16

                    @pl.when(p >= 4)
                    def _():
                        written(p - 4).wait()

                    for h in range(2):
                        ost[p % 4, :, h * half : (h + 1) * half] = nat[h, pl.ds(8, cols)].astype(BF16)
                    written(p).start()

        return c

    def stage(n, c):
        for m in range(4):

            @pl.when(inner & (n == 2 * m) & (m < parts))
            def _(m=m):
                pass_relay(m)

        @pl.when(jnp.where(polar, (n < 8) & ((n % 2 == 1) | (n >= 2 * parts)), (n % 2 == 1) & (n < 2 * parts)))
        def _():
            filter_unit(n)

        @pl.when(polar & (n == 1))
        def _():
            send_group(3)

        @pl.when(n == 2)
        def _():
            spread_winds()

        @pl.when(polar & (n >= 7) & (n < 11))
        def _():
            pass_on(n - 7)

        @pl.when(n == 8)
        def _():
            all_wind_first().wait()
            for e in range(8):
                to_first(7 - e).wait_recv()

        @pl.when((n == 6) & inner)
        def _():
            def give(p, c):
                to_last(p).start()
                return c

            lax.fori_loop(8, 16, give, 0)

        @pl.when((n == 11) & has_last)
        def _():
            all_wind_last().wait()
            for e in range(8, 16):
                to_last(23 - e).wait_recv()

        begin, end = 0, 0
        for when, lo, hi in SWEEP:
            begin, end = jnp.where(n == when, lo, begin), jnp.where(n == when, hi, end)
        lax.fori_loop(begin, end, advance, 0)
        return c

    lax.fori_loop(0, 12, stage, 0)

    for p in range(12, 16):
        written(p).wait()

    @pl.when(polar)
    def _():
        for n in range(8):

            @pl.when(jnp.logical_not(shared(n)))
            def _(n=n):
                for k in (1, 2, 3):
                    forward(n, k)[0].wait_send()
                    returned(n, k).wait_send()

            if n % 2 == 0:

                @pl.when(shared(n))
                def _(n=n):
                    for k in TURN:
                        forward(n, k)[1].wait_send()

    @pl.when(inner)
    def _():
        for m in range(4):

            @pl.when(m < parts)
            def _(m=m):
                for k in (1, 2, 3):
                    relay_copy(m, k).wait_send()
                for k in range(4):
                    returned(2 * m + 1, k).wait_send()

    for p in range(8):
        to_first(p).wait_send()

    @pl.when(has_last)
    def _():
        for p in range(8, 16):
            to_last(p).wait_send()


def per_device(state, winds, decay, widths):
    rows, cols, chans = state.shape
    levels = winds.shape[2] // 2
    half = 2 * levels
    bands = lax.axis_size("lat")
    pad = cols + 24
    seg = (cols + 2 * HALO) // 8
    deep = rows + 2 * HALO
    dma = pltpu.SemaphoreType.DMA
    vm = pltpu.VMEM
    hbm = pl.BlockSpec(memory_space=pl.ANY)
    smem = pl.BlockSpec(memory_space=pltpu.SMEM)
    return pl.pallas_call(
        functools.partial(band_kernel, (bands, rows, cols, pad, levels, seg)),
        out_shape=jax.ShapeDtypeStruct((rows, cols, chans), BF16),
        in_specs=[hbm, hbm, smem, smem],
        out_specs=hbm,
        scratch_shapes=[
            vm((LOADS, cols, chans), F32),
            vm((rows, 2, cols, half), BF16),
            vm((8, 4, cols, half), BF16),
            vm((4, 4, cols, half), BF16),
            vm((4, cols, pad), F32),
            vm((4, 4, cols, pad), BF16),
            vm((4, cols, pad), BF16),
            vm((4, pad, chans), BF16),
            vm((4 * cols + 24, half), F32),
            vm((8, 4, seg, 8, half), BF16),
            vm((deep, 2, seg, 8, half), BF16),
            vm((deep, seg, 8, half), BF16),
            vm((rows, cols, half), BF16),
            vm((2, pad, half), F32),
            vm((2, rows, 16, half), BF16),
            vm((2, rows, 16, half), BF16),
            vm((2, rows, 2, 16, half), BF16),
            vm((2, rows, 2, 16, half), BF16),
            *[vm((FIELD_ROWS, 2, seg + 4, 8, half), F32)] * STEPS,
            vm((WEIGHT_ROWS, 9, seg, 8, half), F32),
            vm((2, pad, half), F32),
            vm((4, cols, chans), BF16),
            dma((LOADS,)), dma((8, 4)), dma((8, 4)), dma((4, 4)), dma((4, 4)), dma((8, 4)), dma((16, 2)),
            dma((16,)), dma((16,)), dma((5,)), dma((4,)), dma((4,)), dma((4,)),
        ],
        compiler_params=pltpu.CompilerParams(
            collective_id=0, has_side_effects=True, vmem_limit_bytes=60 * 2**20
        ),
        name="filter_and_advect",
    )(state, winds, decay, widths)


def solution(mesh):
    in_specs = (P("lat", "lon", None), P("lat", "lon", None), P(), P())
    out_specs = P("lat", "lon", None)
    return jax.shard_map(
        per_device, mesh=mesh, in_specs=in_specs, out_specs=out_specs, check_vma=False
    )
```

```python
import functools

import jax
import jax.numpy as jnp
from jax import lax
from jax.experimental import pallas as pl
from jax.experimental.pallas import tpu as pltpu
from jax.sharding import PartitionSpec as P

STEPS = 4
HALO = 2 * STEPS
MESH = pl.DeviceIdType.MESH
F32 = jnp.float32
BF16 = jnp.bfloat16
FAR = 1.0e6
FIELD_ROWS = 6
WEIGHT_ROWS = 7
TURN = (2, 1, 3, 0)
SHARED = 3
SHARED_EDGE = 1
SWEEP = ((9, 0, 10), (10, 10, 16), (11, 16, 20), (12, 20, 32))
LOADS = 8


def chunks(count, size):
    return [(a, min(size, count - a)) for a in range(0, count, size)]


def band_kernel(
    dims, state, winds, decay, widths, out,
    stf, low, circ, relay, gaps, table, mat, xs, yc, ot, ext, wext, wv, wide,
    wedge, wland, eedge, eland, f0, f1, f2, f3, weights, nat, ost,
    ld, fs, fr, rl, rls, rs, rr, hs, hr, wsem, esem, wrow, osem,
):
    bands, rows, cols, pad, levels, seg = dims
    half = 2 * levels
    lat = lax.axis_index("lat")
    lon = lax.axis_index("lon")
    quarter = bands // 4
    polar = (lat < quarter) | (lat >= bands - quarter)
    inner = jnp.logical_not(polar)
    twin = jnp.where((lat // quarter) % 2 == 0, lat + quarter, lat - quarter)
    home = jnp.where(polar, lat, twin)
    edge = (home // 2 == quarter // 2 - 1) | (home // 2 == (bands - quarter) // 2)
    parts = jnp.where(edge, SHARED_EDGE, SHARED)
    down = (lat + 1) % 2
    home_down = (home + 1) % 2
    first = lat - 1 + 2 * down
    last = lat + 1 - 2 * down
    has_last = (last >= 0) & (last < bands)

    def at(la, lo):
        return {"lat": la, "lon": lo}

    def actual(p, flip):
        return jnp.where(flip == 1, rows - 1 - p, p)

    def remote(src, dst, send, recv, la, lo):
        return pltpu.make_async_remote_copy(
            src_ref=src, dst_ref=dst, send_sem=send, recv_sem=recv, device_id=at(la, lo), device_id_type=MESH
        )

    barrier = pltpu.get_barrier_semaphore()
    for k in range(4):
        pl.semaphore_signal(barrier, inc=1, device_id=at(twin, (lon + k) % 4), device_id_type=MESH)
        if k:
            pl.semaphore_signal(barrier, inc=1, device_id=at(lat, (lon + k) % 4), device_id_type=MESH)
    for side in (1, bands - 1):
        pl.semaphore_signal(barrier, inc=1, device_id=at((lat + side) % bands, lon), device_id_type=MESH)

    def nth_row(n):
        group, place = n // 4, n % 4
        q = jnp.where(group == 1, 2, jnp.where(group == 2, 1, group))
        k = jnp.where(place == 0, 2, jnp.where(place == 1, 1, jnp.where(place == 2, 3, 0)))
        return actual(4 * q + (lon + k) % 4, down)

    def load(n):
        return pltpu.make_async_copy(state.at[nth_row(n)], stf.at[n % LOADS], ld.at[n % LOADS])

    for n in range(LOADS):
        load(n).start()
    wind_load = pltpu.make_async_copy(winds, wv, wsem.at[0])
    wind_load.start()

    pl.semaphore_wait(barrier, 9)

    def convert(n, c):
        load(n).wait()
        i = nth_row(n)
        for h in range(2):
            lanes = slice(h * half, (h + 1) * half)
            low[i, h] = stf[n % LOADS, :, lanes].astype(BF16)
            eedge[0, i, h] = stf[n % LOADS, 0:16, lanes].astype(BF16)
            eedge[1, i, h] = stf[n % LOADS, cols - 16 : cols, lanes].astype(BF16)

        @pl.when(n + LOADS < rows)
        def _():
            load(n + LOADS).start()

        return c

    def shared(u):
        return parts > u - 4

    def forward(u, k):
        q, h = u // 2, u % 2
        target = (lon + k) % 4
        src = low.at[actual(4 * q + target, down), h]
        slot = u if u < 4 else u - parts
        if k == 0:
            own = pltpu.make_async_copy(src, circ.at[slot, lon], fr.at[slot, lon])
        else:
            own = remote(src, circ.at[slot, lon], fs.at[u, k], fr.at[slot, lon], lat, target)
        if u < 4:
            return own, None
        return own, remote(src, relay.at[u - 4, target], fs.at[u, k], rl.at[u - 4, target], twin, lon)

    def send_own(units):
        for u in units:

            @pl.when(jnp.logical_not(shared(u)) if u >= 4 else polar)
            def _(u=u):
                for k in TURN:
                    forward(u, k)[0].start()

    def send_shared(units):
        for u in units:

            @pl.when(shared(u))
            def _(u=u):
                for k in TURN:
                    forward(u, k)[1].start()

    for n, (own, other) in enumerate((((0, 1), ()), ((), (4, 5)), ((2, 3), ()), ((), (6, 7)))):
        lax.fori_loop(4 * n, 4 * n + 4, convert, 0)

        @pl.when(polar)
        def _(own=own, other=other):
            send_own(own)
            send_shared(other)

    wind_load.wait()
    wedge[0] = wv[:, 0:16, :]
    wedge[1] = wv[:, cols - 16 : cols, :]

    def beside(n):
        return (lon + (3 if n == 0 else 1)) % 4

    def wind_edge(n):
        return remote(wedge.at[n], wland.at[n], wsem.at[1 + n], wsem.at[3 + n], lat, beside(n))

    def state_edge(n):
        return remote(eedge.at[n], eland.at[n], esem.at[n], esem.at[2 + n], lat, beside(n))

    for n in range(2):
        wind_edge(n).start()

    @pl.when(inner)
    def _():
        for n in range(2):
            state_edge(n).start()

    there = lax.broadcasted_iota(jnp.int32, (cols, pad), 0)
    here_ = lax.broadcasted_iota(jnp.int32, (cols, pad), 1)
    for d in range(4):
        apart = jnp.abs(there - here_ - d * cols)
        apart = jnp.minimum(apart, 4 * cols - apart).astype(F32)
        gaps[d] = jnp.where(here_ < cols, apart, FAR)

    def tabulate(n, c):
        f, d = n // 4, n % 4
        table[f, d] = jnp.exp(-decay[f] * gaps[d]).astype(BF16)
        return c

    lax.fori_loop(0, 16, tabulate, 0)
    for d in range(4):
        xs[d, pl.ds(pad - 32, 32)] = jnp.zeros((32, 4 * levels), BF16)

    @pl.when(jnp.logical_not(has_last))
    def _():
        ext[rows + HALO : rows + 2 * HALO] = jnp.zeros((HALO, 2, seg, 8, half), BF16)
        wext[rows + HALO : rows + 2 * HALO] = jnp.zeros((HALO, seg, 8, half), BF16)

    def wind_row(i, c):
        wide[0, 0:8] = wland[1, i, 8:16, :].astype(F32)
        wide[0, pl.ds(8, cols)] = wv[i].astype(F32)
        wide[0, pl.ds(8 + cols, 16)] = wland[0, i].astype(F32)
        e = HALO + actual(i, down)
        for j in range(seg):
            wext[e, j] = wide[0, pl.ds(j, 8, stride=seg)].astype(BF16)
        return c

    def wind_first(p):
        return remote(wext.at[HALO + p], wext.at[7 - p], wrow.at[0], wrow.at[1], first, lon)

    def wind_last(p):
        return remote(wext.at[HALO + p], wext.at[39 - p], wrow.at[2], wrow.at[3], last, lon)

    def all_wind_first():
        return remote(wext.at[pl.ds(8, 8)], wext.at[pl.ds(0, 8)], wrow.at[0], wrow.at[1], first, lon)

    def all_wind_last():
        return remote(wext.at[pl.ds(16, 8)], wext.at[pl.ds(24, 8)], wrow.at[2], wrow.at[3], last, lon)

    def to_first(p):
        return remote(ext.at[HALO + p], ext.at[7 - p], hs.at[p], hr.at[7 - p], first, lon)

    def to_last(p):
        return remote(ext.at[HALO + p], ext.at[39 - p], hs.at[p], hr.at[23 - p], last, lon)

    @pl.when(inner)
    def _():
        for n in range(2):
            state_edge(n).wait()

        def state_row(i, c):
            e = HALO + actual(i, down)
            for h in range(2):
                wide[h, 0:8] = eland[1, i, h, 8:16, :].astype(F32)
                wide[h, pl.ds(8, cols)] = low[i, h].astype(F32)
                wide[h, pl.ds(8 + cols, 16)] = eland[0, i, h].astype(F32)
                for j in range(seg):
                    ext[e, h, j] = wide[h, pl.ds(j, 8, stride=seg)].astype(BF16)
            return c

        lax.fori_loop(0, rows, state_row, 0)

        def give(p, c):
            to_first(p).start()
            return c

        lax.fori_loop(0, 8, give, 0)

    def spread_winds():
        for n in range(2):
            wind_edge(n).wait()
        lax.fori_loop(0, rows, wind_row, 0)

        for p in range(8):
            wind_first(p).start()

        @pl.when(has_last)
        def _():
            for p in range(8, 16):
                wind_last(p).start()

    def relay_copy(m, k):
        target = (lon + k) % 4
        if k == 0:
            return pltpu.make_async_copy(relay.at[m, target], circ.at[m, lon], fr.at[m, lon])
        return remote(relay.at[m, target], circ.at[m, lon], rls.at[m, k], fr.at[m, lon], lat, target)

    def pass_relay(m):
        for k in TURN:
            target = (lon + k) % 4
            pltpu.make_async_copy(low.at[0, 0], relay.at[m, target], rl.at[m, target]).wait()
            relay_copy(m, k).start()

    def placed(slot):
        u = jnp.where(polar, jnp.where(slot < 4, slot, slot + parts), slot + 4)
        return slot, u // 2, u % 2

    def returned(n, k):
        slot, q, h = placed(n)
        p = 4 * q + lon
        return remote(
            ot.at[slot, (lon + k) % 4], ext.at[HALO + p, h], rs.at[slot, k], rr.at[p, h], home, (lon + k) % 4
        )

    def filter_unit(n):
        slot, q, h = placed(n)
        i = actual(4 * q + lon, home_down)
        reach = widths[home * rows + i].astype(F32)
        for t in range(4):
            pltpu.make_async_copy(low.at[0, 0], circ.at[slot, t], fr.at[slot, t]).wait()
        for ff in range(2):
            f = 2 * h + ff
            rate = decay[f]
            total = jnp.zeros((1, 1), F32)
            for d in range(4):
                gap = gaps[d, 0:1]
                kept = jnp.where(gap <= reach, jnp.exp(-rate * gap), 0.0)
                total = total + jnp.sum(kept, axis=1, keepdims=True)
            scale = 1.0 / total
            for d in range(4):
                mat[d] = jnp.where(gaps[d] <= reach, table[f, d].astype(F32), 0.0).astype(BF16)
                xs[d, pl.ds(0, cols)] = jnp.concatenate(
                    [circ[slot, (t + d) % 4, :, ff * levels : (ff + 1) * levels] for t in range(4)], axis=1
                )
            result = jnp.dot(mat[0], xs[0], preferred_element_type=F32)
            for d in range(1, 4):
                result = result + jnp.dot(mat[d], xs[d], preferred_element_type=F32)
            result = result * scale
            for t in range(4):
                yc[pl.ds(8 + t * cols, cols), ff * levels : (ff + 1) * levels] = result[:, t * levels : (t + 1) * levels]
        yc[0:8] = yc[pl.ds(4 * cols, 8)]
        yc[pl.ds(8 + 4 * cols, 16)] = yc[8:24]
        for t in range(4):
            for j in range(seg):
                ot[slot, t, j] = yc[pl.ds(t * cols + j, 8, stride=seg)].astype(BF16)
        for k in (2, 1, 3):
            returned(n, k).start()

        @pl.when(polar)
        def _():
            pltpu.make_async_copy(ot.at[slot, lon], ext.at[HALO + 4 * q + lon, h], rr.at[4 * q + lon, h]).start()

        @pl.when(inner)
        def _():
            returned(n, 0).start()

    def pass_on(q):
        def each(p, c):
            for h in range(2):
                pltpu.make_async_copy(ot.at[0, 0], ext.at[HALO + p, h], rr.at[p, h]).wait()

            @pl.when(p < 8)
            def _():
                to_first(p).start()

            @pl.when((p >= 8) & has_last)
            def _():
                to_last(p).start()

            return c

        lax.fori_loop(4 * q, 4 * q + 4, each, 0)

    fields = (f0, f1, f2, f3)
    upward = 1.0 - 2.0 * down.astype(F32)

    def halo_cells(field, slot, h):
        for n in range(2):
            field[slot, h, n] = pltpu.roll(field[slot, h, seg + n], 1, 0)
            field[slot, h, seg + 2 + n] = pltpu.roll(field[slot, h, 2 + n], 7, 0)

    def written(p):
        return pltpu.make_async_copy(ost.at[p % 4], out.at[actual(p, down)], osem.at[p % 4])

    def advance(r, c):
        slot = lax.rem(r, FIELD_ROWS)
        for h in range(2):
            for a, n in chunks(seg, 8):
                f0[slot, h, pl.ds(2 + a, n)] = ext[r, h, pl.ds(a, n)].astype(F32)
            halo_cells(f0, slot, h)

        @pl.when(r >= 4)
        def _():
            made = lax.rem(r - 2, WEIGHT_ROWS)
            for a, n in chunks(seg, 8):
                both = wext[r - 2, pl.ds(a, n)].astype(F32)
                lane = lax.broadcasted_iota(jnp.int32, (n, 8, half), 2)
                other = pltpu.roll(both, levels, 2)
                cu = jnp.where(lane < levels, both, other)
                cv = jnp.where(lane < levels, other, both)
                pairs = ((cu, cu * cu), (cv * upward, cv * cv))
                for m, (one, square) in enumerate(pairs):
                    near, near2 = (2.0 / 3.0) * one, (2.0 / 3.0) * square
                    far, far2 = (1.0 / 12.0) * one, (1.0 / 24.0) * square
                    for w, value in enumerate((near2 - near, far - far2, near2 + near, -far - far2)):
                        weights[made, 4 * m + w, pl.ds(a, n)] = value
                weights[made, 8, pl.ds(a, n)] = 1.0 - 1.25 * (pairs[0][1] + pairs[1][1])

        for s in range(1, STEPS + 1):

            @pl.when(r >= 4 * s)
            def _(s=s):
                old = fields[s - 1]
                i = r - 2 * s
                wrow_ = lax.rem(i, WEIGHT_ROWS)
                here, ahead, ahead2 = (lax.rem(i + o, FIELD_ROWS) for o in (0, 1, 2))
                behind2, behind = (lax.rem(i + o, FIELD_ROWS) for o in (4, 5))
                for a, n in chunks(seg, 4):
                    w = [weights[wrow_, m, pl.ds(a, n)] for m in range(9)]
                    for h in range(2):

                        def cell(row, shift):
                            return old[row, h, pl.ds(2 + a + shift, n)]

                        along = (w[0] * cell(here, 1) + w[1] * cell(here, 2)) + (
                            w[2] * cell(here, -1) + w[3] * cell(here, -2)
                        )
                        across = (w[4] * cell(ahead, 0) + w[5] * cell(ahead2, 0)) + (
                            w[6] * cell(behind, 0) + w[7] * cell(behind2, 0)
                        )
                        value = w[8] * cell(here, 0) + (along + across)
                        if s < STEPS:
                            fields[s][here, h, pl.ds(2 + a, n)] = value
                        else:
                            for m in range(n):
                                nat[h, pl.ds(a + m, 8, stride=seg)] = value[m]
                if s < STEPS:
                    for h in range(2):
                        halo_cells(fields[s], here, h)
                else:
                    p = r - 16

                    @pl.when(p >= 4)
                    def _():
                        written(p - 4).wait()

                    for h in range(2):
                        ost[p % 4, :, h * half : (h + 1) * half] = nat[h, pl.ds(8, cols)].astype(BF16)
                    written(p).start()

        return c

    def stage(n, c):
        for m in range(4):

            @pl.when(inner & (n == 2 * m) & (m < parts))
            def _(m=m):
                pass_relay(m)

        @pl.when(jnp.where(polar, n < 8 - parts, (n % 2 == 1) & (n < 2 * parts)))
        def _():
            filter_unit(jnp.where(polar, n, n // 2))

        @pl.when(polar & (n == 1))
        def _():
            send_own((4, 5, 6, 7))

        @pl.when(n == 1)
        def _():
            spread_winds()

        @pl.when(polar & (n >= 8) & (n < 12))
        def _():
            pass_on(n - 8)

        @pl.when(n == 9)
        def _():
            all_wind_first().wait()
            for e in range(8):
                to_first(7 - e).wait_recv()

        @pl.when((n == 6) & inner)
        def _():
            def give(p, c):
                to_last(p).start()
                return c

            lax.fori_loop(8, 16, give, 0)

        @pl.when((n == 12) & has_last)
        def _():
            all_wind_last().wait()
            for e in range(8, 16):
                to_last(23 - e).wait_recv()

        begin, end = 0, 0
        for when, lo, hi in SWEEP:
            begin, end = jnp.where(n == when, lo, begin), jnp.where(n == when, hi, end)
        lax.fori_loop(begin, end, advance, 0)
        return c

    lax.fori_loop(0, 13, stage, 0)

    for p in range(12, 16):
        written(p).wait()

    @pl.when(polar)
    def _():
        for u in range(8):

            @pl.when(jnp.logical_not(shared(u)) if u >= 4 else polar)
            def _(u=u):
                for k in (1, 2, 3):
                    forward(u, k)[0].wait_send()
                    returned(u if u < 4 else u - parts, k).wait_send()

            if u >= 4:

                @pl.when(shared(u))
                def _(u=u):
                    for k in TURN:
                        forward(u, k)[1].wait_send()

    @pl.when(inner)
    def _():
        for m in range(4):

            @pl.when(m < parts)
            def _(m=m):
                for k in (1, 2, 3):
                    relay_copy(m, k).wait_send()
                for k in range(4):
                    returned(m, k).wait_send()

    for p in range(8):
        to_first(p).wait_send()

    @pl.when(has_last)
    def _():
        for p in range(8, 16):
            to_last(p).wait_send()


def per_device(state, winds, decay, widths):
    rows, cols, chans = state.shape
    levels = winds.shape[2] // 2
    half = 2 * levels
    bands = lax.axis_size("lat")
    pad = cols + 24
    seg = (cols + 2 * HALO) // 8
    deep = rows + 2 * HALO
    dma = pltpu.SemaphoreType.DMA
    vm = pltpu.VMEM
    hbm = pl.BlockSpec(memory_space=pl.ANY)
    smem = pl.BlockSpec(memory_space=pltpu.SMEM)
    return pl.pallas_call(
        functools.partial(band_kernel, (bands, rows, cols, pad, levels, seg)),
        out_shape=jax.ShapeDtypeStruct((rows, cols, chans), BF16),
        in_specs=[hbm, hbm, smem, smem],
        out_specs=hbm,
        scratch_shapes=[
            vm((LOADS, cols, chans), F32),
            vm((rows, 2, cols, half), BF16),
            vm((8, 4, cols, half), BF16),
            vm((4, 4, cols, half), BF16),
            vm((4, cols, pad), F32),
            vm((4, 4, cols, pad), BF16),
            vm((4, cols, pad), BF16),
            vm((4, pad, chans), BF16),
            vm((4 * cols + 24, half), F32),
            vm((8, 4, seg, 8, half), BF16),
            vm((deep, 2, seg, 8, half), BF16),
            vm((deep, seg, 8, half), BF16),
            vm((rows, cols, half), BF16),
            vm((2, pad, half), F32),
            vm((2, rows, 16, half), BF16),
            vm((2, rows, 16, half), BF16),
            vm((2, rows, 2, 16, half), BF16),
            vm((2, rows, 2, 16, half), BF16),
            *[vm((FIELD_ROWS, 2, seg + 4, 8, half), F32)] * STEPS,
            vm((WEIGHT_ROWS, 9, seg, 8, half), F32),
            vm((2, pad, half), F32),
            vm((4, cols, chans), BF16),
            dma((LOADS,)), dma((8, 4)), dma((8, 4)), dma((4, 4)), dma((4, 4)), dma((8, 4)), dma((16, 2)),
            dma((16,)), dma((16,)), dma((5,)), dma((4,)), dma((4,)), dma((4,)),
        ],
        compiler_params=pltpu.CompilerParams(
            collective_id=0, has_side_effects=True, vmem_limit_bytes=60 * 2**20
        ),
        name="filter_and_advect",
    )(state, winds, decay, widths)


def solution(mesh):
    in_specs = (P("lat", "lon", None), P("lat", "lon", None), P(), P())
    out_specs = P("lat", "lon", None)
    return jax.shard_map(
        per_device, mesh=mesh, in_specs=in_specs, out_specs=out_specs, check_vma=False
    )
```

```python
import functools

import jax
import jax.numpy as jnp
from jax import lax
from jax.experimental import pallas as pl
from jax.experimental.pallas import tpu as pltpu
from jax.sharding import PartitionSpec as P

STEPS = 4
HALO = 2 * STEPS
MESH = pl.DeviceIdType.MESH
F32 = jnp.float32
BF16 = jnp.bfloat16
FAR = 1.0e6
FIELD_ROWS = 6
WEIGHT_ROWS = 7
TURN = (2, 1, 3, 0)
SHARED = 3
SHARED_EDGE = 1
SWEEP = ((8, 0, 8), (9, 8, 14), (10, 14, 20), (11, 20, 32))
LOADS = 8


def chunks(count, size):
    return [(a, min(size, count - a)) for a in range(0, count, size)]


def band_kernel(
    dims, state, winds, decay, widths, out,
    stf, low, circ, relay, gaps, table, mat, xs, yc, ot, ext, wext, wv, wide,
    wedge, wland, eedge, eland, f0, f1, f2, f3, weights, nat, ost,
    ld, fs, fr, rl, rls, rs, rr, hs, hr, wsem, esem, wrow, osem,
):
    bands, rows, cols, pad, levels, seg = dims
    half = 2 * levels
    lat = lax.axis_index("lat")
    lon = lax.axis_index("lon")
    quarter = bands // 4
    polar = (lat < quarter) | (lat >= bands - quarter)
    inner = jnp.logical_not(polar)
    twin = jnp.where((lat // quarter) % 2 == 0, lat + quarter, lat - quarter)
    home = jnp.where(polar, lat, twin)
    edge = (home // 2 == quarter // 2 - 1) | (home // 2 == (bands - quarter) // 2)
    parts = jnp.where(edge, SHARED_EDGE, SHARED)
    down = (lat + 1) % 2
    home_down = (home + 1) % 2
    first = lat - 1 + 2 * down
    last = lat + 1 - 2 * down
    has_last = (last >= 0) & (last < bands)

    def at(la, lo):
        return {"lat": la, "lon": lo}

    def actual(p, flip):
        return jnp.where(flip == 1, rows - 1 - p, p)

    def remote(src, dst, send, recv, la, lo):
        return pltpu.make_async_remote_copy(
            src_ref=src, dst_ref=dst, send_sem=send, recv_sem=recv, device_id=at(la, lo), device_id_type=MESH
        )

    barrier = pltpu.get_barrier_semaphore()
    for k in range(4):
        pl.semaphore_signal(barrier, inc=1, device_id=at(twin, (lon + k) % 4), device_id_type=MESH)
        if k:
            pl.semaphore_signal(barrier, inc=1, device_id=at(lat, (lon + k) % 4), device_id_type=MESH)
    for side in (1, bands - 1):
        pl.semaphore_signal(barrier, inc=1, device_id=at((lat + side) % bands, lon), device_id_type=MESH)

    def nth_row(n):
        q, place = n // 4, n % 4
        k = jnp.where(place == 0, 2, jnp.where(place == 1, 1, jnp.where(place == 2, 3, 0)))
        return actual(4 * q + (lon + k) % 4, down)

    def load(n):
        return pltpu.make_async_copy(state.at[nth_row(n)], stf.at[n % LOADS], ld.at[n % LOADS])

    for n in range(LOADS):
        load(n).start()
    wind_load = pltpu.make_async_copy(winds, wv, wsem.at[0])
    wind_load.start()

    pl.semaphore_wait(barrier, 9)

    def convert(n, c):
        load(n).wait()
        i = nth_row(n)
        for h in range(2):
            lanes = slice(h * half, (h + 1) * half)
            low[i, h] = stf[n % LOADS, :, lanes].astype(BF16)
            eedge[0, i, h] = stf[n % LOADS, 0:16, lanes].astype(BF16)
            eedge[1, i, h] = stf[n % LOADS, cols - 16 : cols, lanes].astype(BF16)

        @pl.when(n + LOADS < rows)
        def _():
            load(n + LOADS).start()

        return c

    def own_slot(n):
        return n - jnp.minimum(parts, (n + 1) // 2)

    def shared(n):
        return parts > n // 2 if n % 2 == 0 else lat < 0

    def forward(n, k):
        q, h = n // 2, n % 2
        target = (lon + k) % 4
        src = low.at[actual(4 * q + target, down), h]
        slot = own_slot(n)
        if k == 0:
            own = pltpu.make_async_copy(src, circ.at[slot, lon], fr.at[slot, lon])
        else:
            own = remote(src, circ.at[slot, lon], fs.at[n, k], fr.at[slot, lon], lat, target)
        if n % 2:
            return own, None
        return own, remote(src, relay.at[n // 2, target], fs.at[n, k], rl.at[n // 2, target], twin, lon)

    def send(units):
        for n in units:

            @pl.when(jnp.logical_not(shared(n)))
            def _(n=n):
                for k in TURN:
                    forward(n, k)[0].start()

            if n % 2 == 0:

                @pl.when(shared(n))
                def _(n=n):
                    for k in TURN:
                        forward(n, k)[1].start()

    def sent(n):
        @pl.when(shared(n))
        def _():
            for k in TURN:
                forward(n, k)[1].wait_send()

    for q in range(2):
        lax.fori_loop(4 * q, 4 * q + 4, convert, 0)

        @pl.when(polar)
        def _(q=q):
            send((0, 1) if q == 0 else (3,))

    wind_load.wait()
    wedge[0] = wv[:, 0:16, :]
    wedge[1] = wv[:, cols - 16 : cols, :]

    def beside(n):
        return (lon + (3 if n == 0 else 1)) % 4

    def wind_edge(n):
        return remote(wedge.at[n], wland.at[n], wsem.at[1 + n], wsem.at[3 + n], lat, beside(n))

    def state_edge(n):
        return remote(eedge.at[n], eland.at[n], esem.at[n], esem.at[2 + n], lat, beside(n))

    for n in range(2):
        wind_edge(n).start()

    lax.fori_loop(8, 16, convert, 0)

    @pl.when(inner)
    def _():
        for n in range(2):
            state_edge(n).start()

    there = lax.broadcasted_iota(jnp.int32, (cols, pad), 0)
    here_ = lax.broadcasted_iota(jnp.int32, (cols, pad), 1)
    for d in range(4):
        apart = jnp.abs(there - here_ - d * cols)
        apart = jnp.minimum(apart, 4 * cols - apart).astype(F32)
        gaps[d] = jnp.where(here_ < cols, apart, FAR)

    def tabulate(n, c):
        f, d = n // 4, n % 4
        table[f, d] = jnp.exp(-decay[f] * gaps[d]).astype(BF16)
        return c

    lax.fori_loop(0, 16, tabulate, 0)
    for d in range(4):
        xs[d, pl.ds(pad - 32, 32)] = jnp.zeros((32, 4 * levels), BF16)

    @pl.when(jnp.logical_not(has_last))
    def _():
        ext[rows + HALO : rows + 2 * HALO] = jnp.zeros((HALO, 2, seg, 8, half), BF16)
        wext[rows + HALO : rows + 2 * HALO] = jnp.zeros((HALO, seg, 8, half), BF16)

    def wind_row(i, c):
        wide[0, 0:8] = wland[1, i, 8:16, :].astype(F32)
        wide[0, pl.ds(8, cols)] = wv[i].astype(F32)
        wide[0, pl.ds(8 + cols, 16)] = wland[0, i].astype(F32)
        e = HALO + actual(i, down)
        for j in range(seg):
            wext[e, j] = wide[0, pl.ds(j, 8, stride=seg)].astype(BF16)
        return c

    def wind_first(p):
        return remote(wext.at[HALO + p], wext.at[7 - p], wrow.at[0], wrow.at[1], first, lon)

    def wind_last(p):
        return remote(wext.at[HALO + p], wext.at[39 - p], wrow.at[2], wrow.at[3], last, lon)

    def all_wind_first():
        return remote(wext.at[pl.ds(8, 8)], wext.at[pl.ds(0, 8)], wrow.at[0], wrow.at[1], first, lon)

    def all_wind_last():
        return remote(wext.at[pl.ds(16, 8)], wext.at[pl.ds(24, 8)], wrow.at[2], wrow.at[3], last, lon)

    def to_first(p):
        return remote(ext.at[HALO + p], ext.at[7 - p], hs.at[p], hr.at[7 - p], first, lon)

    def to_last(p):
        return remote(ext.at[HALO + p], ext.at[39 - p], hs.at[p], hr.at[23 - p], last, lon)

    @pl.when(inner)
    def _():
        for n in range(2):
            state_edge(n).wait()

        def state_row(i, c):
            e = HALO + actual(i, down)
            for h in range(2):
                wide[h, 0:8] = eland[1, i, h, 8:16, :].astype(F32)
                wide[h, pl.ds(8, cols)] = low[i, h].astype(F32)
                wide[h, pl.ds(8 + cols, 16)] = eland[0, i, h].astype(F32)
                for j in range(seg):
                    ext[e, h, j] = wide[h, pl.ds(j, 8, stride=seg)].astype(BF16)
            return c

        lax.fori_loop(0, rows, state_row, 0)

        def give(p, c):
            to_first(p).start()
            return c

        lax.fori_loop(0, 8, give, 0)

    def spread_winds():
        for n in range(2):
            wind_edge(n).wait()
        lax.fori_loop(0, rows, wind_row, 0)

        for p in range(8):
            wind_first(p).start()

        @pl.when(has_last)
        def _():
            for p in range(8, 16):
                wind_last(p).start()

    def relay_copy(m, k):
        target = (lon + k) % 4
        if k == 0:
            return pltpu.make_async_copy(relay.at[m, target], circ.at[m, lon], fr.at[m, lon])
        return remote(relay.at[m, target], circ.at[m, lon], rls.at[m, k], fr.at[m, lon], lat, target)

    def pass_relay(m):
        for k in TURN:
            target = (lon + k) % 4
            pltpu.make_async_copy(low.at[0, 0], relay.at[m, target], rl.at[m, target]).wait()
            relay_copy(m, k).start()

    def placed(n):
        slot = jnp.where(polar, n - jnp.minimum(parts, (n + 1) // 2), (n - 1) // 2)
        return slot, n // 2, jnp.where(polar, n % 2, 0)

    def returned(n, k):
        slot, q, h = placed(n)
        p = 4 * q + lon
        return remote(
            ot.at[slot, (lon + k) % 4], ext.at[HALO + p, h], rs.at[slot, k], rr.at[p, h], home, (lon + k) % 4
        )

    def filter_unit(n):
        slot, q, h = placed(n)
        i = actual(4 * q + lon, home_down)
        reach = widths[home * rows + i].astype(F32)
        for t in range(4):
            pltpu.make_async_copy(low.at[0, 0], circ.at[slot, t], fr.at[slot, t]).wait()
        for ff in range(2):
            f = 2 * h + ff
            rate = decay[f]
            total = jnp.zeros((1, 1), F32)
            for d in range(4):
                gap = gaps[d, 0:1]
                kept = jnp.where(gap <= reach, jnp.exp(-rate * gap), 0.0)
                total = total + jnp.sum(kept, axis=1, keepdims=True)
            scale = 1.0 / total
            for d in range(4):
                mat[d] = jnp.where(gaps[d] <= reach, table[f, d].astype(F32), 0.0).astype(BF16)
                xs[d, pl.ds(0, cols)] = jnp.concatenate(
                    [circ[slot, (t + d) % 4, :, ff * levels : (ff + 1) * levels] for t in range(4)], axis=1
                )
            result = jnp.dot(mat[0], xs[0], preferred_element_type=F32)
            for d in range(1, 4):
                result = result + jnp.dot(mat[d], xs[d], preferred_element_type=F32)
            result = result * scale
            for t in range(4):
                yc[pl.ds(8 + t * cols, cols), ff * levels : (ff + 1) * levels] = result[:, t * levels : (t + 1) * levels]
        yc[0:8] = yc[pl.ds(4 * cols, 8)]
        yc[pl.ds(8 + 4 * cols, 16)] = yc[8:24]
        for t in range(4):
            for j in range(seg):
                ot[slot, t, j] = yc[pl.ds(t * cols + j, 8, stride=seg)].astype(BF16)
        for k in (2, 1, 3):
            returned(n, k).start()

        @pl.when(polar)
        def _():
            pltpu.make_async_copy(ot.at[slot, lon], ext.at[HALO + 4 * q + lon, h], rr.at[4 * q + lon, h]).start()

        @pl.when(inner)
        def _():
            returned(n, 0).start()

    def pass_on(q):
        def each(p, c):
            for h in range(2):
                pltpu.make_async_copy(ot.at[0, 0], ext.at[HALO + p, h], rr.at[p, h]).wait()

            @pl.when(p < 8)
            def _():
                to_first(p).start()

            @pl.when((p >= 8) & has_last)
            def _():
                to_last(p).start()

            return c

        lax.fori_loop(4 * q, 4 * q + 4, each, 0)

    fields = (f0, f1, f2, f3)
    upward = 1.0 - 2.0 * down.astype(F32)

    def halo_cells(field, slot, h):
        for n in range(2):
            field[slot, h, n] = pltpu.roll(field[slot, h, seg + n], 1, 0)
            field[slot, h, seg + 2 + n] = pltpu.roll(field[slot, h, 2 + n], 7, 0)

    def written(p):
        return pltpu.make_async_copy(ost.at[p % 4], out.at[actual(p, down)], osem.at[p % 4])

    def advance(r, c):
        slot = lax.rem(r, FIELD_ROWS)
        for h in range(2):
            for a, n in chunks(seg, 8):
                f0[slot, h, pl.ds(2 + a, n)] = ext[r, h, pl.ds(a, n)].astype(F32)
            halo_cells(f0, slot, h)

        @pl.when(r >= 4)
        def _():
            made = lax.rem(r - 2, WEIGHT_ROWS)
            for a, n in chunks(seg, 8):
                both = wext[r - 2, pl.ds(a, n)].astype(F32)
                lane = lax.broadcasted_iota(jnp.int32, (n, 8, half), 2)
                other = pltpu.roll(both, levels, 2)
                cu = jnp.where(lane < levels, both, other)
                cv = jnp.where(lane < levels, other, both)
                pairs = ((cu, cu * cu), (cv * upward, cv * cv))
                for m, (one, square) in enumerate(pairs):
                    near, near2 = (2.0 / 3.0) * one, (2.0 / 3.0) * square
                    far, far2 = (1.0 / 12.0) * one, (1.0 / 24.0) * square
                    for w, value in enumerate((near2 - near, far - far2, near2 + near, -far - far2)):
                        weights[made, 4 * m + w, pl.ds(a, n)] = value
                weights[made, 8, pl.ds(a, n)] = 1.0 - 1.25 * (pairs[0][1] + pairs[1][1])

        for s in range(1, STEPS + 1):

            @pl.when(r >= 4 * s)
            def _(s=s):
                old = fields[s - 1]
                i = r - 2 * s
                wrow_ = lax.rem(i, WEIGHT_ROWS)
                here, ahead, ahead2 = (lax.rem(i + o, FIELD_ROWS) for o in (0, 1, 2))
                behind2, behind = (lax.rem(i + o, FIELD_ROWS) for o in (4, 5))
                for a, n in chunks(seg, 4):
                    w = [weights[wrow_, m, pl.ds(a, n)] for m in range(9)]
                    for h in range(2):

                        def cell(row, shift):
                            return old[row, h, pl.ds(2 + a + shift, n)]

                        along = (w[0] * cell(here, 1) + w[1] * cell(here, 2)) + (
                            w[2] * cell(here, -1) + w[3] * cell(here, -2)
                        )
                        across = (w[4] * cell(ahead, 0) + w[5] * cell(ahead2, 0)) + (
                            w[6] * cell(behind, 0) + w[7] * cell(behind2, 0)
                        )
                        value = w[8] * cell(here, 0) + (along + across)
                        if s < STEPS:
                            fields[s][here, h, pl.ds(2 + a, n)] = value
                        else:
                            for m in range(n):
                                nat[h, pl.ds(a + m, 8, stride=seg)] = value[m]
                if s < STEPS:
                    for h in range(2):
                        halo_cells(fields[s], here, h)
                else:
                    p = r - 16

                    @pl.when(p >= 4)
                    def _():
                        written(p - 4).wait()

                    for h in range(2):
                        ost[p % 4, :, h * half : (h + 1) * half] = nat[h, pl.ds(8, cols)].astype(BF16)
                    written(p).start()

        return c

    def stage(n, c):
        @pl.when(n == jnp.where(polar, 4, 0))
        def _():
            spread_winds()

        for m in range(4):

            @pl.when(inner & (n == 2 * m) & (m < parts))
            def _(m=m):
                pass_relay(m)

        @pl.when(jnp.where(polar, (n < 8) & ((n % 2 == 1) | (n >= 2 * parts)), (n % 2 == 1) & (n < 2 * parts)))
        def _():
            filter_unit(n)

        @pl.when(polar & (n == 1))
        def _():
            sent(0)
            send((2,))

        @pl.when(polar & (n == 3))
        def _():
            send((5,))
            sent(2)
            send((4, 6, 7))

        @pl.when(polar & (n >= 7) & (n < 11))
        def _():
            pass_on(n - 7)

        @pl.when(n == 8)
        def _():
            all_wind_first().wait()
            for e in range(8):
                to_first(7 - e).wait_recv()

        @pl.when((n == 6) & inner)
        def _():
            def give(p, c):
                to_last(p).start()
                return c

            lax.fori_loop(8, 16, give, 0)

        @pl.when((n == 11) & has_last)
        def _():
            all_wind_last().wait()
            for e in range(8, 16):
                to_last(23 - e).wait_recv()

        begin, end = 0, 0
        for when, lo, hi in SWEEP:
            begin, end = jnp.where(n == when, lo, begin), jnp.where(n == when, hi, end)
        lax.fori_loop(begin, end, advance, 0)
        return c

    lax.fori_loop(0, 12, stage, 0)

    for p in range(12, 16):
        written(p).wait()

    @pl.when(polar)
    def _():
        for n in range(8):

            @pl.when(jnp.logical_not(shared(n)))
            def _(n=n):
                for k in (1, 2, 3):
                    forward(n, k)[0].wait_send()
                    returned(n, k).wait_send()

            if n in (4, 6):
                sent(n)

    @pl.when(inner)
    def _():
        for m in range(4):

            @pl.when(m < parts)
            def _(m=m):
                for k in (1, 2, 3):
                    relay_copy(m, k).wait_send()
                for k in range(4):
                    returned(2 * m + 1, k).wait_send()

    for p in range(8):
        to_first(p).wait_send()

    @pl.when(has_last)
    def _():
        for p in range(8, 16):
            to_last(p).wait_send()


def per_device(state, winds, decay, widths):
    rows, cols, chans = state.shape
    levels = winds.shape[2] // 2
    half = 2 * levels
    bands = lax.axis_size("lat")
    pad = cols + 24
    seg = (cols + 2 * HALO) // 8
    deep = rows + 2 * HALO
    dma = pltpu.SemaphoreType.DMA
    vm = pltpu.VMEM
    hbm = pl.BlockSpec(memory_space=pl.ANY)
    smem = pl.BlockSpec(memory_space=pltpu.SMEM)
    return pl.pallas_call(
        functools.partial(band_kernel, (bands, rows, cols, pad, levels, seg)),
        out_shape=jax.ShapeDtypeStruct((rows, cols, chans), BF16),
        in_specs=[hbm, hbm, smem, smem],
        out_specs=hbm,
        scratch_shapes=[
            vm((LOADS, cols, chans), F32),
            vm((rows, 2, cols, half), BF16),
            vm((8, 4, cols, half), BF16),
            vm((4, 4, cols, half), BF16),
            vm((4, cols, pad), F32),
            vm((4, 4, cols, pad), BF16),
            vm((4, cols, pad), BF16),
            vm((4, pad, chans), BF16),
            vm((4 * cols + 24, half), F32),
            vm((8, 4, seg, 8, half), BF16),
            vm((deep, 2, seg, 8, half), BF16),
            vm((deep, seg, 8, half), BF16),
            vm((rows, cols, half), BF16),
            vm((2, pad, half), F32),
            vm((2, rows, 16, half), BF16),
            vm((2, rows, 16, half), BF16),
            vm((2, rows, 2, 16, half), BF16),
            vm((2, rows, 2, 16, half), BF16),
            *[vm((FIELD_ROWS, 2, seg + 4, 8, half), F32)] * STEPS,
            vm((WEIGHT_ROWS, 9, seg, 8, half), F32),
            vm((2, pad, half), F32),
            vm((4, cols, chans), BF16),
            dma((LOADS,)), dma((8, 4)), dma((8, 4)), dma((4, 4)), dma((4, 4)), dma((8, 4)), dma((16, 2)),
            dma((16,)), dma((16,)), dma((5,)), dma((4,)), dma((4,)), dma((4,)),
        ],
        compiler_params=pltpu.CompilerParams(
            collective_id=0, has_side_effects=True, vmem_limit_bytes=60 * 2**20
        ),
        name="filter_and_advect",
    )(state, winds, decay, widths)


def solution(mesh):
    in_specs = (P("lat", "lon", None), P("lat", "lon", None), P(), P())
    out_specs = P("lat", "lon", None)
    return jax.shard_map(
        per_device, mesh=mesh, in_specs=in_specs, out_specs=out_specs, check_vma=False
    )
```

```python
import functools

import jax
import jax.numpy as jnp
from jax import lax
from jax.experimental import pallas as pl
from jax.experimental.pallas import tpu as pltpu
from jax.sharding import PartitionSpec as P

STEPS = 4
HALO = 2 * STEPS
MESH = pl.DeviceIdType.MESH
F32 = jnp.float32
BF16 = jnp.bfloat16
FAR = 1.0e6
FIELD_ROWS = 6
WEIGHT_ROWS = 7
TURN = (2, 1, 3, 0)
SHARED = 3
SHARED_EDGE = 2
SWEEP = ((8, 0, 8), (9, 8, 14), (10, 14, 20), (11, 20, 32))
LOADS = 8


def chunks(count, size):
    return [(a, min(size, count - a)) for a in range(0, count, size)]


def band_kernel(
    dims, state, winds, decay, widths, out,
    stf, low, circ, relay, gaps, table, mat, xs, yc, ot, ext, wext, wv, wide,
    wedge, wland, eedge, eland, f0, f1, f2, f3, weights, nat, ost,
    ld, fs, fr, rl, rls, rs, rr, hs, hr, wsem, esem, wrow, osem,
):
    bands, rows, cols, pad, levels, seg = dims
    half = 2 * levels
    lat = lax.axis_index("lat")
    lon = lax.axis_index("lon")
    quarter = bands // 4
    polar = (lat < quarter) | (lat >= bands - quarter)
    inner = jnp.logical_not(polar)
    twin = jnp.where((lat // quarter) % 2 == 0, lat + quarter, lat - quarter)
    home = jnp.where(polar, lat, twin)
    edge = (home // 2 == quarter // 2 - 1) | (home // 2 == (bands - quarter) // 2)
    parts = jnp.where(edge, SHARED_EDGE, SHARED)
    down = (lat + 1) % 2
    home_down = (home + 1) % 2
    first = lat - 1 + 2 * down
    last = lat + 1 - 2 * down
    has_last = (last >= 0) & (last < bands)

    def at(la, lo):
        return {"lat": la, "lon": lo}

    def actual(p, flip):
        return jnp.where(flip == 1, rows - 1 - p, p)

    def remote(src, dst, send, recv, la, lo):
        return pltpu.make_async_remote_copy(
            src_ref=src, dst_ref=dst, send_sem=send, recv_sem=recv, device_id=at(la, lo), device_id_type=MESH
        )

    barrier = pltpu.get_barrier_semaphore()
    for k in range(4):
        pl.semaphore_signal(barrier, inc=1, device_id=at(twin, (lon + k) % 4), device_id_type=MESH)
        if k:
            pl.semaphore_signal(barrier, inc=1, device_id=at(lat, (lon + k) % 4), device_id_type=MESH)
    for side in (1, bands - 1):
        pl.semaphore_signal(barrier, inc=1, device_id=at((lat + side) % bands, lon), device_id_type=MESH)

    def nth_row(n):
        q, place = n // 4, n % 4
        k = jnp.where(place == 0, 2, jnp.where(place == 1, 1, jnp.where(place == 2, 3, 0)))
        return actual(4 * q + (lon + k) % 4, down)

    def load(n):
        return pltpu.make_async_copy(state.at[nth_row(n)], stf.at[n % LOADS], ld.at[n % LOADS])

    for n in range(LOADS):
        load(n).start()
    wind_load = pltpu.make_async_copy(winds, wv, wsem.at[0])
    wind_load.start()

    pl.semaphore_wait(barrier, 9)

    def convert(n, c):
        load(n).wait()
        i = nth_row(n)
        for h in range(2):
            lanes = slice(h * half, (h + 1) * half)
            low[i, h] = stf[n % LOADS, :, lanes].astype(BF16)
            eedge[0, i, h] = stf[n % LOADS, 0:16, lanes].astype(BF16)
            eedge[1, i, h] = stf[n % LOADS, cols - 16 : cols, lanes].astype(BF16)

        @pl.when(n + LOADS < rows)
        def _():
            load(n + LOADS).start()

        return c

    def own_slot(n):
        return n - jnp.minimum(parts, (n + 1) // 2)

    def shared(n):
        return parts > n // 2 if n % 2 == 0 else lat < 0

    def forward(n, k):
        q, h = n // 2, n % 2
        target = (lon + k) % 4
        src = low.at[actual(4 * q + target, down), h]
        slot = own_slot(n)
        if k == 0:
            own = pltpu.make_async_copy(src, circ.at[slot, lon], fr.at[slot, lon])
        else:
            own = remote(src, circ.at[slot, lon], fs.at[n, k], fr.at[slot, lon], lat, target)
        if n % 2:
            return own, None
        return own, remote(src, relay.at[n // 2, target], fs.at[n, k], rl.at[n // 2, target], twin, lon)

    def send_group(q):
        for n in (2 * q, 2 * q + 1):

            @pl.when(jnp.logical_not(shared(n)))
            def _(n=n):
                for k in TURN:
                    forward(n, k)[0].start()

            if n % 2 == 0:

                @pl.when(shared(n))
                def _(n=n):
                    for k in TURN:
                        forward(n, k)[1].start()

    for q in range(2):
        lax.fori_loop(4 * q, 4 * q + 4, convert, 0)

        @pl.when(polar)
        def _(q=q):
            send_group(q)

    wind_load.wait()
    wedge[0] = wv[:, 0:16, :]
    wedge[1] = wv[:, cols - 16 : cols, :]

    def beside(n):
        return (lon + (3 if n == 0 else 1)) % 4

    def wind_edge(n):
        return remote(wedge.at[n], wland.at[n], wsem.at[1 + n], wsem.at[3 + n], lat, beside(n))

    def state_edge(n):
        return remote(eedge.at[n], eland.at[n], esem.at[n], esem.at[2 + n], lat, beside(n))

    for n in range(2):
        wind_edge(n).start()

    lax.fori_loop(8, 16, convert, 0)

    @pl.when(inner)
    def _():
        for n in range(2):
            state_edge(n).start()

    there = lax.broadcasted_iota(jnp.int32, (cols, pad), 0)
    here_ = lax.broadcasted_iota(jnp.int32, (cols, pad), 1)
    for d in range(4):
        apart = jnp.abs(there - here_ - d * cols)
        apart = jnp.minimum(apart, 4 * cols - apart).astype(F32)
        gaps[d] = jnp.where(here_ < cols, apart, FAR)

    def tabulate(n, c):
        f, d = n // 4, n % 4
        table[f, d] = jnp.exp(-decay[f] * gaps[d]).astype(BF16)
        return c

    lax.fori_loop(0, 16, tabulate, 0)
    for d in range(4):
        xs[d, pl.ds(pad - 32, 32)] = jnp.zeros((32, 4 * levels), BF16)

    @pl.when(polar)
    def _():
        send_group(2)

    @pl.when(jnp.logical_not(has_last))
    def _():
        ext[rows + HALO : rows + 2 * HALO] = jnp.zeros((HALO, 2, seg, 8, half), BF16)
        wext[rows + HALO : rows + 2 * HALO] = jnp.zeros((HALO, seg, 8, half), BF16)

    def wind_row(i, c):
        wide[0, 0:8] = wland[1, i, 8:16, :].astype(F32)
        wide[0, pl.ds(8, cols)] = wv[i].astype(F32)
        wide[0, pl.ds(8 + cols, 16)] = wland[0, i].astype(F32)
        e = HALO + actual(i, down)
        for j in range(seg):
            wext[e, j] = wide[0, pl.ds(j, 8, stride=seg)].astype(BF16)
        return c

    def wind_first(p):
        return remote(wext.at[HALO + p], wext.at[7 - p], wrow.at[0], wrow.at[1], first, lon)

    def wind_last(p):
        return remote(wext.at[HALO + p], wext.at[39 - p], wrow.at[2], wrow.at[3], last, lon)

    def all_wind_first():
        return remote(wext.at[pl.ds(8, 8)], wext.at[pl.ds(0, 8)], wrow.at[0], wrow.at[1], first, lon)

    def all_wind_last():
        return remote(wext.at[pl.ds(16, 8)], wext.at[pl.ds(24, 8)], wrow.at[2], wrow.at[3], last, lon)

    def to_first(p):
        return remote(ext.at[HALO + p], ext.at[7 - p], hs.at[p], hr.at[7 - p], first, lon)

    def to_last(p):
        return remote(ext.at[HALO + p], ext.at[39 - p], hs.at[p], hr.at[23 - p], last, lon)

    @pl.when(inner)
    def _():
        for n in range(2):
            state_edge(n).wait()

        def state_row(i, c):
            e = HALO + actual(i, down)
            for h in range(2):
                wide[h, 0:8] = eland[1, i, h, 8:16, :].astype(F32)
                wide[h, pl.ds(8, cols)] = low[i, h].astype(F32)
                wide[h, pl.ds(8 + cols, 16)] = eland[0, i, h].astype(F32)
                for j in range(seg):
                    ext[e, h, j] = wide[h, pl.ds(j, 8, stride=seg)].astype(BF16)
            return c

        lax.fori_loop(0, rows, state_row, 0)

        def give(p, c):
            to_first(p).start()
            to_last(p + 8).start()
            return c

        lax.fori_loop(0, 8, give, 0)

    def spread_winds():
        for n in range(2):
            wind_edge(n).wait()
        lax.fori_loop(0, rows, wind_row, 0)

        for p in range(8):
            wind_first(p).start()

        @pl.when(has_last)
        def _():
            for p in range(8, 16):
                wind_last(p).start()

    def relay_copy(m, k):
        target = (lon + k) % 4
        if k == 0:
            return pltpu.make_async_copy(relay.at[m, target], circ.at[m, lon], fr.at[m, lon])
        return remote(relay.at[m, target], circ.at[m, lon], rls.at[m, k], fr.at[m, lon], lat, target)

    def pass_relay(m):
        for k in TURN:
            target = (lon + k) % 4
            pltpu.make_async_copy(low.at[0, 0], relay.at[m, target], rl.at[m, target]).wait()
            relay_copy(m, k).start()

    def placed(n):
        slot = jnp.where(polar, n - jnp.minimum(parts, (n + 1) // 2), (n - 1) // 2)
        return slot, n // 2, jnp.where(polar, n % 2, 0)

    def returned(n, k):
        slot, q, h = placed(n)
        p = 4 * q + lon
        return remote(
            ot.at[slot, (lon + k) % 4], ext.at[HALO + p, h], rs.at[slot, k], rr.at[p, h], home, (lon + k) % 4
        )

    def filter_unit(n):
        slot, q, h = placed(n)
        i = actual(4 * q + lon, home_down)
        reach = widths[home * rows + i].astype(F32)
        for t in range(4):
            pltpu.make_async_copy(low.at[0, 0], circ.at[slot, t], fr.at[slot, t]).wait()
        for ff in range(2):
            f = 2 * h + ff
            rate = decay[f]
            total = jnp.zeros((1, 1), F32)
            for d in range(4):
                gap = gaps[d, 0:1]
                kept = jnp.where(gap <= reach, jnp.exp(-rate * gap), 0.0)
                total = total + jnp.sum(kept, axis=1, keepdims=True)
            scale = 1.0 / total
            for d in range(4):
                mat[d] = jnp.where(gaps[d] <= reach, table[f, d].astype(F32), 0.0).astype(BF16)
                xs[d, pl.ds(0, cols)] = jnp.concatenate(
                    [circ[slot, (t + d) % 4, :, ff * levels : (ff + 1) * levels] for t in range(4)], axis=1
                )
            result = jnp.dot(mat[0], xs[0], preferred_element_type=F32)
            for d in range(1, 4):
                result = result + jnp.dot(mat[d], xs[d], preferred_element_type=F32)
            result = result * scale
            for t in range(4):
                yc[pl.ds(8 + t * cols, cols), ff * levels : (ff + 1) * levels] = result[:, t * levels : (t + 1) * levels]
        yc[0:8] = yc[pl.ds(4 * cols, 8)]
        yc[pl.ds(8 + 4 * cols, 16)] = yc[8:24]
        for t in range(4):
            for j in range(seg):
                ot[slot, t, j] = yc[pl.ds(t * cols + j, 8, stride=seg)].astype(BF16)
        for k in (2, 1, 3):
            returned(n, k).start()

        @pl.when(polar)
        def _():
            pltpu.make_async_copy(ot.at[slot, lon], ext.at[HALO + 4 * q + lon, h], rr.at[4 * q + lon, h]).start()

        @pl.when(inner)
        def _():
            returned(n, 0).start()

    def pass_on(q):
        def each(p, c):
            for h in range(2):
                pltpu.make_async_copy(ot.at[0, 0], ext.at[HALO + p, h], rr.at[p, h]).wait()

            @pl.when(p < 8)
            def _():
                to_first(p).start()

            @pl.when((p >= 8) & has_last)
            def _():
                to_last(p).start()

            return c

        lax.fori_loop(4 * q, 4 * q + 4, each, 0)

    fields = (f0, f1, f2, f3)
    upward = 1.0 - 2.0 * down.astype(F32)

    def halo_cells(field, slot, h):
        for n in range(2):
            field[slot, h, n] = pltpu.roll(field[slot, h, seg + n], 1, 0)
            field[slot, h, seg + 2 + n] = pltpu.roll(field[slot, h, 2 + n], 7, 0)

    def written(p):
        return pltpu.make_async_copy(ost.at[p % 4], out.at[actual(p, down)], osem.at[p % 4])

    def advance(r, c):
        slot = lax.rem(r, FIELD_ROWS)
        for h in range(2):
            for a, n in chunks(seg, 8):
                f0[slot, h, pl.ds(2 + a, n)] = ext[r, h, pl.ds(a, n)].astype(F32)
            halo_cells(f0, slot, h)

        @pl.when(r >= 4)
        def _():
            made = lax.rem(r - 2, WEIGHT_ROWS)
            for a, n in chunks(seg, 8):
                both = wext[r - 2, pl.ds(a, n)].astype(F32)
                lane = lax.broadcasted_iota(jnp.int32, (n, 8, half), 2)
                other = pltpu.roll(both, levels, 2)
                cu = jnp.where(lane < levels, both, other)
                cv = jnp.where(lane < levels, other, both)
                pairs = ((cu, cu * cu), (cv * upward, cv * cv))
                for m, (one, square) in enumerate(pairs):
                    near, near2 = (2.0 / 3.0) * one, (2.0 / 3.0) * square
                    far, far2 = (1.0 / 12.0) * one, (1.0 / 24.0) * square
                    for w, value in enumerate((near2 - near, far - far2, near2 + near, -far - far2)):
                        weights[made, 4 * m + w, pl.ds(a, n)] = value
                weights[made, 8, pl.ds(a, n)] = 1.0 - 1.25 * (pairs[0][1] + pairs[1][1])

        for s in range(1, STEPS + 1):

            @pl.when(r >= 4 * s)
            def _(s=s):
                old = fields[s - 1]
                i = r - 2 * s
                wrow_ = lax.rem(i, WEIGHT_ROWS)
                here, ahead, ahead2 = (lax.rem(i + o, FIELD_ROWS) for o in (0, 1, 2))
                behind2, behind = (lax.rem(i + o, FIELD_ROWS) for o in (4, 5))
                for a, n in chunks(seg, 4):
                    w = [weights[wrow_, m, pl.ds(a, n)] for m in range(9)]
                    for h in range(2):

                        def cell(row, shift):
                            return old[row, h, pl.ds(2 + a + shift, n)]

                        along = (w[0] * cell(here, 1) + w[1] * cell(here, 2)) + (
                            w[2] * cell(here, -1) + w[3] * cell(here, -2)
                        )
                        across = (w[4] * cell(ahead, 0) + w[5] * cell(ahead2, 0)) + (
                            w[6] * cell(behind, 0) + w[7] * cell(behind2, 0)
                        )
                        value = w[8] * cell(here, 0) + (along + across)
                        if s < STEPS:
                            fields[s][here, h, pl.ds(2 + a, n)] = value
                        else:
                            for m in range(n):
                                nat[h, pl.ds(a + m, 8, stride=seg)] = value[m]
                if s < STEPS:
                    for h in range(2):
                        halo_cells(fields[s], here, h)
                else:
                    p = r - 16

                    @pl.when(p >= 4)
                    def _():
                        written(p - 4).wait()

                    for h in range(2):
                        ost[p % 4, :, h * half : (h + 1) * half] = nat[h, pl.ds(8, cols)].astype(BF16)
                    written(p).start()

        return c

    def stage(n, c):
        for m in range(4):

            @pl.when(inner & (n == 2 * m) & (m < parts))
            def _(m=m):
                pass_relay(m)

        @pl.when(jnp.where(polar, (n < 8) & ((n % 2 == 1) | (n >= 2 * parts)), (n % 2 == 1) & (n < 2 * parts)))
        def _():
            filter_unit(n)

        @pl.when(polar & (n == 1))
        def _():
            send_group(3)

        @pl.when(n == 2)
        def _():
            spread_winds()

        @pl.when(polar & (n >= 7) & (n < 11))
        def _():
            pass_on(n - 7)

        @pl.when(n == 8)
        def _():
            all_wind_first().wait()
            for e in range(8):
                to_first(7 - e).wait_recv()

        @pl.when((n == 11) & has_last)
        def _():
            all_wind_last().wait()
            for e in range(8, 16):
                to_last(23 - e).wait_recv()

        begin, end = 0, 0
        for when, lo, hi in SWEEP:
            begin, end = jnp.where(n == when, lo, begin), jnp.where(n == when, hi, end)
        lax.fori_loop(begin, end, advance, 0)
        return c

    lax.fori_loop(0, 12, stage, 0)

    for p in range(12, 16):
        written(p).wait()

    @pl.when(polar)
    def _():
        for n in range(8):

            @pl.when(jnp.logical_not(shared(n)))
            def _(n=n):
                for k in (1, 2, 3):
                    forward(n, k)[0].wait_send()
                    returned(n, k).wait_send()

            if n % 2 == 0:

                @pl.when(shared(n))
                def _(n=n):
                    for k in TURN:
                        forward(n, k)[1].wait_send()

    @pl.when(inner)
    def _():
        for m in range(4):

            @pl.when(m < parts)
            def _(m=m):
                for k in (1, 2, 3):
                    relay_copy(m, k).wait_send()
                for k in range(4):
                    returned(2 * m + 1, k).wait_send()

    for p in range(8):
        to_first(p).wait_send()

    @pl.when(has_last)
    def _():
        for p in range(8, 16):
            to_last(p).wait_send()


def per_device(state, winds, decay, widths):
    rows, cols, chans = state.shape
    levels = winds.shape[2] // 2
    half = 2 * levels
    bands = lax.axis_size("lat")
    pad = cols + 24
    seg = (cols + 2 * HALO) // 8
    deep = rows + 2 * HALO
    dma = pltpu.SemaphoreType.DMA
    vm = pltpu.VMEM
    hbm = pl.BlockSpec(memory_space=pl.ANY)
    smem = pl.BlockSpec(memory_space=pltpu.SMEM)
    return pl.pallas_call(
        functools.partial(band_kernel, (bands, rows, cols, pad, levels, seg)),
        out_shape=jax.ShapeDtypeStruct((rows, cols, chans), BF16),
        in_specs=[hbm, hbm, smem, smem],
        out_specs=hbm,
        scratch_shapes=[
            vm((LOADS, cols, chans), F32),
            vm((rows, 2, cols, half), BF16),
            vm((8, 4, cols, half), BF16),
            vm((4, 4, cols, half), BF16),
            vm((4, cols, pad), F32),
            vm((4, 4, cols, pad), BF16),
            vm((4, cols, pad), BF16),
            vm((4, pad, chans), BF16),
            vm((4 * cols + 24, half), F32),
            vm((8, 4, seg, 8, half), BF16),
            vm((deep, 2, seg, 8, half), BF16),
            vm((deep, seg, 8, half), BF16),
            vm((rows, cols, half), BF16),
            vm((2, pad, half), F32),
            vm((2, rows, 16, half), BF16),
            vm((2, rows, 16, half), BF16),
            vm((2, rows, 2, 16, half), BF16),
            vm((2, rows, 2, 16, half), BF16),
            *[vm((FIELD_ROWS, 2, seg + 4, 8, half), F32)] * STEPS,
            vm((WEIGHT_ROWS, 9, seg, 8, half), F32),
            vm((2, pad, half), F32),
            vm((4, cols, chans), BF16),
            dma((LOADS,)), dma((8, 4)), dma((8, 4)), dma((4, 4)), dma((4, 4)), dma((8, 4)), dma((16, 2)),
            dma((16,)), dma((16,)), dma((5,)), dma((4,)), dma((4,)), dma((4,)),
        ],
        compiler_params=pltpu.CompilerParams(
            collective_id=0, has_side_effects=True, vmem_limit_bytes=60 * 2**20
        ),
        name="filter_and_advect",
    )(state, winds, decay, widths)


def solution(mesh):
    in_specs = (P("lat", "lon", None), P("lat", "lon", None), P(), P())
    out_specs = P("lat", "lon", None)
    return jax.shard_map(
        per_device, mesh=mesh, in_specs=in_specs, out_specs=out_specs, check_vma=False
    )
```

```python
import functools

import jax
import jax.numpy as jnp
from jax import lax
from jax.experimental import pallas as pl
from jax.experimental.pallas import tpu as pltpu
from jax.sharding import PartitionSpec as P

STEPS = 4
HALO = 2 * STEPS
MESH = pl.DeviceIdType.MESH
F32 = jnp.float32
BF16 = jnp.bfloat16
FAR = 1.0e6
FIELD_ROWS = 6
WEIGHT_ROWS = 7
TURN = (2, 1, 3, 0)
SHARED = 3
SHARED_EDGE = 1
SWEEP = ((8, 0, 8), (9, 8, 14), (10, 14, 20), (11, 20, 32))
LOADS = 8


def chunks(count, size):
    return [(a, min(size, count - a)) for a in range(0, count, size)]


def band_kernel(
    dims, state, winds, decay, widths, out,
    stf, low, circ, relay, gaps, table, mat, xs, yc, ot, ext, wext, wv, wide,
    wedge, wland, eedge, eland, f0, f1, f2, f3, weights, nat, ost,
    ld, fs, fr, rl, rls, rs, rr, hs, hr, wsem, esem, wrow, osem,
):
    bands, rows, cols, pad, levels, seg = dims
    half = 2 * levels
    lat = lax.axis_index("lat")
    lon = lax.axis_index("lon")
    quarter = bands // 4
    polar = (lat < quarter) | (lat >= bands - quarter)
    inner = jnp.logical_not(polar)
    twin = jnp.where((lat // quarter) % 2 == 0, lat + quarter, lat - quarter)
    home = jnp.where(polar, lat, twin)
    edge = (home // 2 == quarter // 2 - 1) | (home // 2 == (bands - quarter) // 2)
    parts = jnp.where(edge, SHARED_EDGE, SHARED)
    down = (lat + 1) % 2
    home_down = (home + 1) % 2
    first = lat - 1 + 2 * down
    last = lat + 1 - 2 * down
    has_last = (last >= 0) & (last < bands)

    def at(la, lo):
        return {"lat": la, "lon": lo}

    def actual(p, flip):
        return jnp.where(flip == 1, rows - 1 - p, p)

    def remote(src, dst, send, recv, la, lo):
        return pltpu.make_async_remote_copy(
            src_ref=src, dst_ref=dst, send_sem=send, recv_sem=recv, device_id=at(la, lo), device_id_type=MESH
        )

    barrier = pltpu.get_barrier_semaphore()
    for k in range(4):
        pl.semaphore_signal(barrier, inc=1, device_id=at(twin, (lon + k) % 4), device_id_type=MESH)
        if k:
            pl.semaphore_signal(barrier, inc=1, device_id=at(lat, (lon + k) % 4), device_id_type=MESH)
    for side in (1, bands - 1):
        pl.semaphore_signal(barrier, inc=1, device_id=at((lat + side) % bands, lon), device_id_type=MESH)

    def nth_row(n):
        q, place = n // 4, n % 4
        k = jnp.where(place == 0, 2, jnp.where(place == 1, 1, jnp.where(place == 2, 3, 0)))
        return actual(4 * q + (lon + k) % 4, down)

    def load(n):
        return pltpu.make_async_copy(state.at[nth_row(n)], stf.at[n % LOADS], ld.at[n % LOADS])

    for n in range(LOADS):
        load(n).start()
    wind_load = pltpu.make_async_copy(winds, wv, wsem.at[0])
    wind_load.start()

    pl.semaphore_wait(barrier, 9)

    def convert(n, c):
        load(n).wait()
        i = nth_row(n)
        for h in range(2):
            lanes = slice(h * half, (h + 1) * half)
            low[i, h] = stf[n % LOADS, :, lanes].astype(BF16)
            eedge[0, i, h] = stf[n % LOADS, 0:16, lanes].astype(BF16)
            eedge[1, i, h] = stf[n % LOADS, cols - 16 : cols, lanes].astype(BF16)

        @pl.when(n + LOADS < rows)
        def _():
            load(n + LOADS).start()

        return c

    def own_slot(n):
        return n - jnp.minimum(parts, (n + 1) // 2)

    def shared(n):
        return parts > n // 2 if n % 2 == 0 else lat < 0

    def forward(n, k):
        q, h = n // 2, n % 2
        target = (lon + k) % 4
        src = low.at[actual(4 * q + target, down), h]
        slot = own_slot(n)
        if k == 0:
            own = pltpu.make_async_copy(src, circ.at[slot, lon], fr.at[slot, lon])
        else:
            own = remote(src, circ.at[slot, lon], fs.at[n, k], fr.at[slot, lon], lat, target)
        if n % 2:
            return own, None
        return own, remote(src, relay.at[n // 2, target], fs.at[n, k], rl.at[n // 2, target], twin, lon)

    def send_group(q):
        for n in (2 * q, 2 * q + 1):

            @pl.when(jnp.logical_not(shared(n)))
            def _(n=n):
                for k in TURN:
                    forward(n, k)[0].start()

            if n % 2 == 0:

                @pl.when(shared(n))
                def _(n=n):
                    for k in TURN:
                        forward(n, k)[1].start()

    for q in range(2):
        lax.fori_loop(4 * q, 4 * q + 4, convert, 0)

        @pl.when(polar)
        def _(q=q):
            send_group(q)

    wind_load.wait()
    wedge[0] = wv[:, 0:16, :]
    wedge[1] = wv[:, cols - 16 : cols, :]

    def beside(n):
        return (lon + (3 if n == 0 else 1)) % 4

    def wind_edge(n):
        return remote(wedge.at[n], wland.at[n], wsem.at[1 + n], wsem.at[3 + n], lat, beside(n))

    def state_edge(n):
        return remote(eedge.at[n], eland.at[n], esem.at[n], esem.at[2 + n], lat, beside(n))

    for n in range(2):
        wind_edge(n).start()

    lax.fori_loop(8, 16, convert, 0)

    @pl.when(inner)
    def _():
        for n in range(2):
            state_edge(n).start()

    there = lax.broadcasted_iota(jnp.int32, (cols, pad), 0)
    here_ = lax.broadcasted_iota(jnp.int32, (cols, pad), 1)
    for d in range(4):
        apart = jnp.abs(there - here_ - d * cols)
        apart = jnp.minimum(apart, 4 * cols - apart).astype(F32)
        gaps[d] = jnp.where(here_ < cols, apart, FAR)

    def tabulate(n, c):
        f, d = n // 4, n % 4
        table[f, d] = jnp.exp(-decay[f] * gaps[d]).astype(BF16)
        return c

    lax.fori_loop(0, 16, tabulate, 0)
    for d in range(4):
        xs[d, pl.ds(pad - 32, 32)] = jnp.zeros((32, 4 * levels), BF16)

    @pl.when(polar)
    def _():
        send_group(2)

    @pl.when(jnp.logical_not(has_last))
    def _():
        ext[rows + HALO : rows + 2 * HALO] = jnp.zeros((HALO, 2, seg, 8, half), BF16)
        wext[rows + HALO : rows + 2 * HALO] = jnp.zeros((HALO, seg, 8, half), BF16)

    def wind_row(i, c):
        wide[0, 0:8] = wland[1, i, 8:16, :].astype(F32)
        wide[0, pl.ds(8, cols)] = wv[i].astype(F32)
        wide[0, pl.ds(8 + cols, 16)] = wland[0, i].astype(F32)
        e = HALO + actual(i, down)
        for j in range(seg):
            wext[e, j] = wide[0, pl.ds(j, 8, stride=seg)].astype(BF16)
        return c

    def wind_first(p):
        return remote(wext.at[HALO + p], wext.at[7 - p], wrow.at[0], wrow.at[1], first, lon)

    def wind_last(p):
        return remote(wext.at[HALO + p], wext.at[39 - p], wrow.at[2], wrow.at[3], last, lon)

    def all_wind_first():
        return remote(wext.at[pl.ds(8, 8)], wext.at[pl.ds(0, 8)], wrow.at[0], wrow.at[1], first, lon)

    def all_wind_last():
        return remote(wext.at[pl.ds(16, 8)], wext.at[pl.ds(24, 8)], wrow.at[2], wrow.at[3], last, lon)

    def to_first(p):
        return remote(ext.at[HALO + p], ext.at[7 - p], hs.at[p], hr.at[7 - p], first, lon)

    def to_last(p):
        return remote(ext.at[HALO + p], ext.at[39 - p], hs.at[p], hr.at[23 - p], last, lon)

    @pl.when(inner)
    def _():
        for n in range(2):
            state_edge(n).wait()

        def state_row(i, c):
            e = HALO + actual(i, down)
            for h in range(2):
                wide[h, 0:8] = eland[1, i, h, 8:16, :].astype(F32)
                wide[h, pl.ds(8, cols)] = low[i, h].astype(F32)
                wide[h, pl.ds(8 + cols, 16)] = eland[0, i, h].astype(F32)
                for j in range(seg):
                    ext[e, h, j] = wide[h, pl.ds(j, 8, stride=seg)].astype(BF16)
            return c

        lax.fori_loop(0, rows, state_row, 0)

        def give(p, c):
            to_first(p).start()
            to_last(p + 8).start()
            return c

        lax.fori_loop(0, 8, give, 0)

    def spread_winds():
        for n in range(2):
            wind_edge(n).wait()
        lax.fori_loop(0, rows, wind_row, 0)

        for p in range(8):
            wind_first(p).start()

        @pl.when(has_last)
        def _():
            for p in range(8, 16):
                wind_last(p).start()

    def relay_copy(m, k):
        target = (lon + k) % 4
        if k == 0:
            return pltpu.make_async_copy(relay.at[m, target], circ.at[m, lon], fr.at[m, lon])
        return remote(relay.at[m, target], circ.at[m, lon], rls.at[m, k], fr.at[m, lon], lat, target)

    def pass_relay(m):
        for k in TURN:
            target = (lon + k) % 4
            pltpu.make_async_copy(low.at[0, 0], relay.at[m, target], rl.at[m, target]).wait()
            relay_copy(m, k).start()

    def placed(n):
        slot = jnp.where(polar, n - jnp.minimum(parts, (n + 1) // 2), (n - 1) // 2)
        return slot, n // 2, jnp.where(polar, n % 2, 0)

    def returned(n, k):
        slot, q, h = placed(n)
        p = 4 * q + lon
        return remote(
            ot.at[slot, (lon + k) % 4], ext.at[HALO + p, h], rs.at[slot, k], rr.at[p, h], home, (lon + k) % 4
        )

    def filter_unit(n):
        slot, q, h = placed(n)
        i = actual(4 * q + lon, home_down)
        reach = widths[home * rows + i].astype(F32)
        for t in range(4):
            pltpu.make_async_copy(low.at[0, 0], circ.at[slot, t], fr.at[slot, t]).wait()
        for ff in range(2):
            f = 2 * h + ff
            rate = decay[f]
            total = jnp.zeros((1, 1), F32)
            for d in range(4):
                gap = gaps[d, 0:1]
                kept = jnp.where(gap <= reach, jnp.exp(-rate * gap), 0.0)
                total = total + jnp.sum(kept, axis=1, keepdims=True)
            scale = 1.0 / total
            for d in range(4):
                mat[d] = jnp.where(gaps[d] <= reach, table[f, d].astype(F32), 0.0).astype(BF16)
                xs[d, pl.ds(0, cols)] = jnp.concatenate(
                    [circ[slot, (t + d) % 4, :, ff * levels : (ff + 1) * levels] for t in range(4)], axis=1
                )
            result = jnp.dot(mat[0], xs[0], preferred_element_type=F32)
            for d in range(1, 4):
                result = result + jnp.dot(mat[d], xs[d], preferred_element_type=F32)
            result = result * scale
            for t in range(4):
                yc[pl.ds(8 + t * cols, cols), ff * levels : (ff + 1) * levels] = result[:, t * levels : (t + 1) * levels]
        yc[0:8] = yc[pl.ds(4 * cols, 8)]
        yc[pl.ds(8 + 4 * cols, 16)] = yc[8:24]
        for t in range(4):
            for j in range(seg):
                ot[slot, t, j] = yc[pl.ds(t * cols + j, 8, stride=seg)].astype(BF16)
        for k in (2, 1, 3):
            returned(n, k).start()

        @pl.when(polar)
        def _():
            pltpu.make_async_copy(ot.at[slot, lon], ext.at[HALO + 4 * q + lon, h], rr.at[4 * q + lon, h]).start()

        @pl.when(inner)
        def _():
            returned(n, 0).start()

    def pass_on(q):
        def each(p, c):
            for h in range(2):
                pltpu.make_async_copy(ot.at[0, 0], ext.at[HALO + p, h], rr.at[p, h]).wait()

            @pl.when(p < 8)
            def _():
                to_first(p).start()

            @pl.when((p >= 8) & has_last)
            def _():
                to_last(p).start()

            return c

        lax.fori_loop(4 * q, 4 * q + 4, each, 0)

    fields = (f0, f1, f2, f3)
    upward = 1.0 - 2.0 * down.astype(F32)

    def halo_cells(field, slot, h):
        for n in range(2):
            field[slot, h, n] = pltpu.roll(field[slot, h, seg + n], 1, 0)
            field[slot, h, seg + 2 + n] = pltpu.roll(field[slot, h, 2 + n], 7, 0)

    def written(p):
        return pltpu.make_async_copy(ost.at[p % 4], out.at[actual(p, down)], osem.at[p % 4])

    def advance(r, c):
        slot = lax.rem(r, FIELD_ROWS)
        for h in range(2):
            for a, n in chunks(seg, 8):
                f0[slot, h, pl.ds(2 + a, n)] = ext[r, h, pl.ds(a, n)].astype(F32)
            halo_cells(f0, slot, h)

        @pl.when(r >= 4)
        def _():
            made = lax.rem(r - 2, WEIGHT_ROWS)
            for a, n in chunks(seg, 8):
                both = wext[r - 2, pl.ds(a, n)].astype(F32)
                lane = lax.broadcasted_iota(jnp.int32, (n, 8, half), 2)
                other = pltpu.roll(both, levels, 2)
                cu = jnp.where(lane < levels, both, other)
                cv = jnp.where(lane < levels, other, both)
                pairs = ((cu, cu * cu), (cv * upward, cv * cv))
                for m, (one, square) in enumerate(pairs):
                    near, near2 = (2.0 / 3.0) * one, (2.0 / 3.0) * square
                    far, far2 = (1.0 / 12.0) * one, (1.0 / 24.0) * square
                    for w, value in enumerate((near2 - near, far - far2, near2 + near, -far - far2)):
                        weights[made, 4 * m + w, pl.ds(a, n)] = value
                weights[made, 8, pl.ds(a, n)] = 1.0 - 1.25 * (pairs[0][1] + pairs[1][1])

        for s in range(1, STEPS + 1):

            @pl.when(r >= 4 * s)
            def _(s=s):
                old = fields[s - 1]
                i = r - 2 * s
                wrow_ = lax.rem(i, WEIGHT_ROWS)
                here, ahead, ahead2 = (lax.rem(i + o, FIELD_ROWS) for o in (0, 1, 2))
                behind2, behind = (lax.rem(i + o, FIELD_ROWS) for o in (4, 5))
                for a, n in chunks(seg, 4):
                    w = [weights[wrow_, m, pl.ds(a, n)] for m in range(9)]
                    for h in range(2):

                        def cell(row, shift):
                            return old[row, h, pl.ds(2 + a + shift, n)]

                        along = (w[0] * cell(here, 1) + w[1] * cell(here, 2)) + (
                            w[2] * cell(here, -1) + w[3] * cell(here, -2)
                        )
                        across = (w[4] * cell(ahead, 0) + w[5] * cell(ahead2, 0)) + (
                            w[6] * cell(behind, 0) + w[7] * cell(behind2, 0)
                        )
                        value = w[8] * cell(here, 0) + (along + across)
                        if s < STEPS:
                            fields[s][here, h, pl.ds(2 + a, n)] = value
                        else:
                            for m in range(n):
                                nat[h, pl.ds(a + m, 8, stride=seg)] = value[m]
                if s < STEPS:
                    for h in range(2):
                        halo_cells(fields[s], here, h)
                else:
                    p = r - 16

                    @pl.when(p >= 4)
                    def _():
                        written(p - 4).wait()

                    for h in range(2):
                        ost[p % 4, :, h * half : (h + 1) * half] = nat[h, pl.ds(8, cols)].astype(BF16)
                    written(p).start()

        return c

    def stage(n, c):
        for m in range(4):

            @pl.when(inner & (n == 2 * m) & (m < parts))
            def _(m=m):
                pass_relay(m)

        @pl.when(jnp.where(polar, (n < 8) & ((n % 2 == 1) | (n >= 2 * parts)), (n % 2 == 1) & (n < 2 * parts)))
        def _():
            filter_unit(n)

        @pl.when(polar & (n == 1))
        def _():
            send_group(3)

        @pl.when(n == 2)
        def _():
            spread_winds()

        @pl.when(polar & (n >= 7) & (n < 11))
        def _():
            pass_on(n - 7)

        @pl.when(n == 8)
        def _():
            all_wind_first().wait()
            for e in range(8):
                to_first(7 - e).wait_recv()

        @pl.when((n == 11) & has_last)
        def _():
            all_wind_last().wait()
            for e in range(8, 16):
                to_last(23 - e).wait_recv()

        begin, end = 0, 0
        for when, lo, hi in SWEEP:
            begin, end = jnp.where(n == when, lo, begin), jnp.where(n == when, hi, end)
        lax.fori_loop(begin, end, advance, 0)
        return c

    lax.fori_loop(0, 12, stage, 0)

    for p in range(12, 16):
        written(p).wait()

    @pl.when(polar)
    def _():
        for n in range(8):

            @pl.when(jnp.logical_not(shared(n)))
            def _(n=n):
                for k in (1, 2, 3):
                    forward(n, k)[0].wait_send()
                    returned(n, k).wait_send()

            if n % 2 == 0:

                @pl.when(shared(n))
                def _(n=n):
                    for k in TURN:
                        forward(n, k)[1].wait_send()

    @pl.when(inner)
    def _():
        for m in range(4):

            @pl.when(m < parts)
            def _(m=m):
                for k in (1, 2, 3):
                    relay_copy(m, k).wait_send()
                for k in range(4):
                    returned(2 * m + 1, k).wait_send()

    for p in range(8):
        to_first(p).wait_send()

    @pl.when(has_last)
    def _():
        for p in range(8, 16):
            to_last(p).wait_send()


def per_device(state, winds, decay, widths):
    rows, cols, chans = state.shape
    levels = winds.shape[2] // 2
    half = 2 * levels
    bands = lax.axis_size("lat")
    pad = cols + 24
    seg = (cols + 2 * HALO) // 8
    deep = rows + 2 * HALO
    dma = pltpu.SemaphoreType.DMA
    vm = pltpu.VMEM
    hbm = pl.BlockSpec(memory_space=pl.ANY)
    smem = pl.BlockSpec(memory_space=pltpu.SMEM)
    return pl.pallas_call(
        functools.partial(band_kernel, (bands, rows, cols, pad, levels, seg)),
        out_shape=jax.ShapeDtypeStruct((rows, cols, chans), BF16),
        in_specs=[hbm, hbm, smem, smem],
        out_specs=hbm,
        scratch_shapes=[
            vm((LOADS, cols, chans), F32),
            vm((rows, 2, cols, half), BF16),
            vm((8, 4, cols, half), BF16),
            vm((4, 4, cols, half), BF16),
            vm((4, cols, pad), F32),
            vm((4, 4, cols, pad), BF16),
            vm((4, cols, pad), BF16),
            vm((4, pad, chans), BF16),
            vm((4 * cols + 24, half), F32),
            vm((8, 4, seg, 8, half), BF16),
            vm((deep, 2, seg, 8, half), BF16),
            vm((deep, seg, 8, half), BF16),
            vm((rows, cols, half), BF16),
            vm((2, pad, half), F32),
            vm((2, rows, 16, half), BF16),
            vm((2, rows, 16, half), BF16),
            vm((2, rows, 2, 16, half), BF16),
            vm((2, rows, 2, 16, half), BF16),
            *[vm((FIELD_ROWS, 2, seg + 4, 8, half), F32)] * STEPS,
            vm((WEIGHT_ROWS, 9, seg, 8, half), F32),
            vm((2, pad, half), F32),
            vm((4, cols, chans), BF16),
            dma((LOADS,)), dma((8, 4)), dma((8, 4)), dma((4, 4)), dma((4, 4)), dma((8, 4)), dma((16, 2)),
            dma((16,)), dma((16,)), dma((5,)), dma((4,)), dma((4,)), dma((4,)),
        ],
        compiler_params=pltpu.CompilerParams(
            collective_id=0, has_side_effects=True, vmem_limit_bytes=60 * 2**20
        ),
        name="filter_and_advect",
    )(state, winds, decay, widths)


def solution(mesh):
    in_specs = (P("lat", "lon", None), P("lat", "lon", None), P(), P())
    out_specs = P("lat", "lon", None)
    return jax.shard_map(
        per_device, mesh=mesh, in_specs=in_specs, out_specs=out_specs, check_vma=False
    )
```
